1024 devices in a mesh: expert: 64 (over y, x), dp: 16 (over z, core).
Axes of the slice: x: 8, y: 8, z: 8, core: 2. Of those that a mesh axis runs over, the one named last changes fastest.
Arguments:
- tokens: bfloat16 [32768, 1024], P(('expert', 'dp')), may hold values from -6 to 6
- out_grad: bfloat16 [32768, 1024], P(('expert', 'dp')), may hold values from -6 to 6
- expert_ids: int32 [32768, 8], P(('expert', 'dp')), may hold values from 0 to 63, all different within a row; in each aligned block of 32 rows (0 to 31, 32 to 63, ...) at most 6 rows name the same one
- gates: bfloat16 [32768, 8], P(('expert', 'dp')), may hold values from 0.019897461 to 0.29882812
- w_gate: bfloat16 [64, 1024, 384], P('expert', 'dp'), may hold values from -0.1875 to 0.1875
- w_up: bfloat16 [64, 1024, 384], P('expert', 'dp'), may hold values from -0.1875 to 0.1875
- w_down: bfloat16 [64, 1024, 384], P('expert', 'dp'), may hold values from -0.3125 to 0.3125
Outputs:
- d_tokens: bfloat16 [32768, 1024], P(('expert', 'dp'))
- d_gates: bfloat16 [32768, 8], P(('expert', 'dp'))
- d_gate_w: float32 [64, 1024, 384], P('expert', 'dp')
- d_up_w: float32 [64, 1024, 384], P('expert', 'dp')
- d_down_w: float32 [64, 1024, 384], P('expert', 'dp')
The draws below stay inside these ranges and needn't reach their ends.
Inputs may be any that keep to these rules, and one draw needn't show every extreme that they name: `expert_ids`: each row names 8 different experts. The rows of one device (aligned blocks of 32 rows) name no expert more than 6 times, and in every draw some device names some expert exactly 6 times.
All inputs are finite; a program needn't handle non-finite values.
Results may differ from the reference program's by a relative error of at most 0.022.
Values may be sent and summed in bfloat16 or wider, within the bound.
A program may use at most 32 MiB of HBM per device.

```python
import math
import jax
import jax.numpy as jnp
import numpy as np
from jax import lax

D = 1024
FF = 384
TOK_DEV = 32
EXPERTS = 64
TOPK = 8
CAP = 6
TOKENS = 32768
N_EXPERT = 64
N_DP = 16


def shard_levels(stream_key, dims, cuts, smallest, high):
    loudness, own = 1.0, jax.random.fold_in(stream_key, 6)
    for dim, shards_of in cuts:
        heights = jnp.exp(jax.random.uniform(jax.random.fold_in(own, dim), (shards_of,), jnp.float32, smallest / len(cuts), high / len(cuts)))
        loudness = loudness * jnp.repeat(heights, dims[dim] // shards_of).reshape([-1 if axis == dim else 1 for axis in range(len(dims))])
    return loudness


def routed_block(own_key, own, number, rows, amount, top, most, slope):
    sequence = jax.random.permutation(own_key, amount)
    heavy_load, usual = portions_of(amount, rows * top, most, slope, True), portions_of(amount, rows * top, most, slope, False)
    places = jnp.arange(amount)

    def named(sizes, turn):
        used = int((sizes > 0).sum())
        fixed = max(1, used // 4)
        moved = fixed + (places - fixed + turn * (used - fixed)) % max(1, amount - fixed)
        return jnp.zeros((amount,), jnp.int32).at[sequence[jnp.where(places < fixed, places, moved)]].set(jnp.asarray(sizes, jnp.int32))

    sizes = jnp.where(number % 4 == 0, named(heavy_load, number // 4), named(usual, number - number // 4 - 1))
    mixed = jax.random.permutation(jax.random.fold_in(own, 3), amount)
    giver, taker = mixed[0:amount // 2 * 2:2], mixed[1:amount // 2 * 2:2]
    margin = jnp.minimum(sizes[giver] - 1, most - sizes[taker]) // 2
    margin = jnp.where((giver == sequence[0]) | (taker == sequence[0]) | (sizes[taker] == 0), 0, jnp.maximum(margin, 0))
    moved = jax.random.randint(jax.random.fold_in(own, 4), (amount // 2,), 0, 1 << 20) % (margin + 1)
    sizes = sizes.at[giver].add(-moved).at[taker].add(moved)
    items = jnp.searchsorted(jnp.cumsum(sizes), jnp.arange(rows * top), side="right").astype(jnp.int32)
    listing = items.reshape(top, rows).T
    listing = listing[jax.random.permutation(jax.random.fold_in(own, 1), rows)]
    turn = jax.random.randint(jax.random.fold_in(own, 2), (rows, 1), 0, top)
    return jnp.take_along_axis(listing, (jnp.arange(top)[None, :] + turn) % top, axis=1)


def portions_of(amount, total, reach, lean, full):
    weights = [(1 << 20) // math.isqrt(rank ** lean) + 1 for rank in range(1, amount + 1)]
    largest = reach if full else min(reach, max(-(-total // amount), total * weights[0] // sum(weights)))
    least = 1 if total - largest >= amount - 1 else 0
    given, rest = [largest] + [least] * (amount - 1), total - largest - least * (amount - 1)
    while rest > 0:
        movable = [i for i in range(1, amount) if given[i] < largest] or [i for i in range(1, amount) if given[i] < reach]
        whole, left = sum([weights[i] for i in movable]), rest
        for i in movable:
            addition = min(reach - given[i], max(1, left * weights[i] // whole), rest)
            given[i] = given[i] + addition
            rest = rest - addition
    return np.array(given)


def bell_draw(rng, extent, width, reach, split=(), held_as=jnp.bfloat16):
    level = shard_levels(rng, extent, split, -0.22, 0.18) if split else 1.0
    values = jax.random.normal(rng, extent, jnp.float32) * width * level
    return jnp.minimum(jnp.maximum(values, -reach), reach).astype(held_as)


def setup_inputs(seed: int = 0) -> dict:
    streams_of = jax.random.split(jax.random.key(seed), 8)
    tokens = bell_draw(streams_of[0], (TOKENS, D), 1.0, 6.0, ((0, 1024),))
    out_grad = bell_draw(streams_of[1], (TOKENS, D), 1.0, 6.0, ((0, 1024),))
    expert_ids_keys = jax.random.split(jax.random.fold_in(streams_of[2], 1), TOKENS // TOK_DEV)
    expert_ids_turns = jax.random.permutation(jax.random.fold_in(streams_of[2], 3), TOKENS // TOK_DEV)
    expert_ids = jax.vmap(lambda own, number: routed_block(jax.random.fold_in(streams_of[2], 2), own, number, TOK_DEV, EXPERTS, TOPK, CAP, 2))(expert_ids_keys, expert_ids_turns).reshape((TOKENS, TOPK))
    gates = jnp.clip(0.019897461 + 0.27893066 * jax.random.uniform(streams_of[3], (TOKENS, TOPK), jnp.float32) ** shard_levels(streams_of[3], (TOKENS, TOPK), ((0, 1024),), -0.2, 0.2), 0.019897461, 0.29882812).astype(jnp.bfloat16)
    w_gate = bell_draw(streams_of[4], (EXPERTS, D, FF), D ** -0.5, 0.1875, ((0, 64), (1, 16)))
    w_up = bell_draw(streams_of[5], (EXPERTS, D, FF), D ** -0.5, 0.1875, ((0, 64), (1, 16)))
    w_down = bell_draw(streams_of[6], (EXPERTS, D, FF), FF ** -0.5, 0.3125, ((0, 64), (1, 16)))
    return dict(tokens=tokens, out_grad=out_grad, expert_ids=expert_ids, gates=gates, w_gate=w_gate, w_up=w_up, w_down=w_down)


def group_partial(left, right):
    summed = jnp.einsum("ndcx,ndcf->dxf", left.astype(jnp.float32), right.astype(jnp.float32))
    rounded = summed.astype(jnp.bfloat16)
    return jnp.sum(rounded.astype(jnp.float32), axis=0)


def reference(tokens, out_grad, expert_ids, gates, w_gate, w_up, w_down):
    blocks = TOKENS // TOK_DEV
    per_block = TOK_DEV * TOPK
    sentinel = TOKENS * TOPK
    block_ids = expert_ids.reshape(blocks, per_block)
    onehot = (block_ids[:, :, None] == jnp.arange(EXPERTS, dtype=jnp.int32)[None, None, :]).astype(jnp.int32)
    earlier = jnp.cumsum(onehot, axis=1) - onehot
    slot_pos = jnp.sum(earlier * onehot, axis=2).astype(jnp.int32)
    block_num = jnp.arange(blocks, dtype=jnp.int32)[:, None]
    target = ((block_num * EXPERTS + block_ids) * CAP + slot_pos).astype(jnp.int32)
    assigned = jnp.arange(sentinel, dtype=jnp.int32)
    slot_table = jnp.full((blocks * EXPERTS * CAP,), sentinel, dtype=jnp.int32)
    slot_table = slot_table.at[target.reshape(-1)].set(assigned)
    slot_table = slot_table.reshape(blocks, EXPERTS, CAP)
    token_pad = jnp.concatenate([tokens, jnp.zeros((1, D), tokens.dtype)], axis=0)
    grad_pad = jnp.concatenate([out_grad, jnp.zeros((1, D), out_grad.dtype)], axis=0)
    gate_pad = jnp.concatenate([gates.reshape(-1), jnp.zeros((1,), gates.dtype)], axis=0)

    def one_expert(carry, expert):
        acc_in, acc_score = carry
        slot_index = lax.dynamic_index_in_dim(slot_table, expert, axis=1, keepdims=False).reshape(-1)
        token_row = (slot_index // TOPK).astype(jnp.int32)
        in_rows = token_pad[token_row]
        grad_rows = grad_pad[token_row]
        gate_rows = gate_pad[slot_index]
        gate_mat = lax.dynamic_index_in_dim(w_gate, expert, axis=0, keepdims=False)
        up_mat = lax.dynamic_index_in_dim(w_up, expert, axis=0, keepdims=False)
        down_mat = lax.dynamic_index_in_dim(w_down, expert, axis=0, keepdims=False)
        gate_pre = jnp.dot(in_rows, gate_mat, preferred_element_type=jnp.float32)
        up_pre = jnp.dot(in_rows, up_mat, preferred_element_type=jnp.float32)
        sig_gate = jax.nn.sigmoid(gate_pre)
        act_gate = gate_pre * sig_gate
        hidden = (act_gate * up_pre).astype(jnp.bfloat16)
        expert_out = jnp.dot(hidden, down_mat.T, preferred_element_type=jnp.float32)
        gate_score = jnp.sum(grad_rows.astype(jnp.float32) * expert_out, axis=1).astype(jnp.bfloat16)
        scaled = (gate_rows.astype(jnp.float32)[:, None] * grad_rows.astype(jnp.float32)).astype(jnp.bfloat16)
        hid_grad = jnp.dot(scaled, down_mat, preferred_element_type=jnp.float32)
        gate_grad = (hid_grad * up_pre * sig_gate * (1.0 + gate_pre * (1.0 - sig_gate))).astype(jnp.bfloat16)
        up_grad = (hid_grad * act_gate).astype(jnp.bfloat16)
        in_grad = jnp.dot(gate_grad, gate_mat.T, preferred_element_type=jnp.float32)
        in_grad = (in_grad + jnp.dot(up_grad, up_mat.T, preferred_element_type=jnp.float32)).astype(jnp.bfloat16)
        acc_in = acc_in.at[token_row].add(in_grad.astype(jnp.float32))
        acc_score = acc_score.at[slot_index].set(gate_score.astype(acc_score.dtype))
        grouped = (N_EXPERT, N_DP, CAP)
        in_four = in_rows.reshape(grouped + (D,))
        scaled_four = scaled.reshape(grouped + (D,))
        gate_w = group_partial(in_four, gate_grad.reshape(grouped + (FF,)))
        up_w = group_partial(in_four, up_grad.reshape(grouped + (FF,)))
        down_w = group_partial(scaled_four, hidden.reshape(grouped + (FF,)))
        return (acc_in, acc_score), (gate_w, up_w, down_w)

    start_carry = (jnp.zeros((TOKENS + 1, D), jnp.float32), jnp.zeros((sentinel + 1,), jnp.float32))
    final_carry, grads = lax.scan(one_expert, start_carry, jnp.arange(EXPERTS, dtype=jnp.int32))
    acc_in, acc_score = final_carry
    d_tokens = acc_in[:TOKENS].astype(jnp.bfloat16)
    d_gates = acc_score[:sentinel].reshape(TOKENS, TOPK).astype(jnp.bfloat16)
    return (d_tokens, d_gates, grads[0], grads[1], grads[2])
```

```python
import functools

import jax
import jax.numpy as jnp
from jax import lax
from jax.experimental import pallas as pl
from jax.experimental.pallas import tpu as pltpu
from jax.sharding import PartitionSpec as P

MESH = pl.DeviceIdType.MESH
LANES = 128


def dot_nn(a, b):
    return lax.dot_general(a, b, (((1,), (0,)), ((), ())), preferred_element_type=jnp.float32)


def dot_nt(a, b):
    return lax.dot_general(a, b, (((1,), (1,)), ((), ())), preferred_element_type=jnp.float32)


def dot_tn(a, b):
    return lax.dot_general(a, b, (((0,), (0,)), ((), ())), preferred_element_type=jnp.float32)


def far_first(line):
    return sorted(range(1, line), key=lambda k: -min(k, line - k))


def kernel(
    line, ring, cap,
    tok_ref, grad_ref, ids_ref, gates_ref, wg_ref, wu_ref, wd_ref,
    dtok_ref, dgate_ref, dwg_ref, dwu_ref, dwd_ref,
    meta, rows1, send2, recv2, wbuf, back_out, back_in, home_out, home_in,
    part, sib, plus_out, plus_in, minus_out, minus_in,
    meta_s, meta_r, one_s, one_r, two_s, two_r, w_s, w_r, ws_s, ws_r,
    back_s, back_r, home_s, home_r, sib_s, sib_r, plus_s, plus_r, minus_s, minus_r,
):
    tok, dim = tok_ref.shape
    top = ids_ref.shape[0]
    hid = wg_ref.shape[1]
    slots = line * cap
    shard = wg_ref.shape[0]

    expert = lax.axis_index("expert")
    dp = lax.axis_index("dp")
    z, c = dp // 2, dp % 2
    stride_a = line - (line - 1) * c
    stride_b = 1 + (line - 1) * c
    y, x = expert // line, expert % line
    a = y * (1 - c) + x * c
    b = x * (1 - c) + y * c

    def on_a(k):
        return (((a + k + line) % line) * stride_a + b * stride_b, dp)

    def on_b(k):
        return (a * stride_a + ((b + k + line) % line) * stride_b, dp)

    def on_z(k):
        return (expert, ((z + k + ring) % ring) * 2 + c)

    sibling = (expert, z * 2 + 1 - c)

    def remote(src, dst, send, recv, target):
        copy = pltpu.make_async_remote_copy(
            src_ref=src, dst_ref=dst, send_sem=send, recv_sem=recv, device_id=target, device_id_type=MESH
        )
        copy.start()
        return copy

    barrier = pltpu.get_barrier_semaphore()
    for k in range(1, line):
        pl.semaphore_signal(barrier, inc=1, device_id=on_a(k), device_id_type=MESH)
        pl.semaphore_signal(barrier, inc=1, device_id=on_b(k), device_id_type=MESH)
    for k in range(1, ring):
        pl.semaphore_signal(barrier, inc=1, device_id=on_z(k), device_id_type=MESH)
    pl.semaphore_signal(barrier, inc=1, device_id=sibling, device_id_type=MESH)

    ids_f = ids_ref[...].astype(jnp.float32)
    gates_f = gates_ref[...].astype(jnp.float32)
    meta[0, :, 0:tok] = jnp.concatenate([ids_f, gates_f], axis=0).astype(jnp.bfloat16)
    meta[0, :, tok:] = jnp.zeros((2 * top, LANES - tok), jnp.bfloat16)
    rows1[0, :, 0:dim] = tok_ref[...]
    rows1[0, :, dim:] = grad_ref[...]
    wbuf[z, c, :, 0:hid] = wg_ref[...]
    wbuf[z, c, :, hid : 2 * hid] = wu_ref[...]
    wbuf[z, c, :, 2 * hid :] = wd_ref[...]

    pl.semaphore_wait(barrier, 2 * (line - 1) + ring)

    pending = []
    metas, ones, weights = {}, {}, {}
    for k in far_first(line):
        metas[k] = remote(meta.at[0], meta.at[k], meta_s.at[k], meta_r.at[k], on_a(k))
    for k in far_first(line):
        ones[k] = remote(rows1.at[0], rows1.at[k], one_s.at[k], one_r.at[k], on_a(k))
    for k in far_first(ring):
        weights[k] = remote(wbuf.at[z, c], wbuf.at[z, c], w_s.at[k], w_r.at[k], on_z(k))
    pending += list(metas.values()) + list(ones.values()) + list(weights.values())

    for k in range(1, line):
        metas[k].wait_recv()
    every = jnp.concatenate([meta[p].astype(jnp.float32)[:, 0:tok] for p in range(line)], axis=1)
    ids_all, gates_all = every[0:top], every[top:]
    total = line * tok
    masks, scales = [], []
    for j in range(line):
        named = (a * stride_a + ((b + j) % line) * stride_b).astype(jnp.float32)
        hit = ids_all == named
        masks.append(jnp.sum(jnp.where(hit, 1.0, 0.0), axis=0, keepdims=True))
        scales.append(jnp.sum(jnp.where(hit, gates_all, 0.0), axis=0, keepdims=True))
    mask = jnp.concatenate(masks, axis=0)
    rows = lax.broadcasted_iota(jnp.int32, (total, total), 0)
    cols = lax.broadcasted_iota(jnp.int32, (total, total), 1)
    earlier = ((rows < cols) & (rows // tok == cols // tok)).astype(jnp.float32).astype(jnp.bfloat16)
    pos = dot_nn(mask.astype(jnp.bfloat16), earlier)
    first = (lax.broadcasted_iota(jnp.int32, (line, total), 1) // tok * cap).astype(jnp.float32)
    place = jnp.where(mask > 0.0, first + pos, -1.0)
    slot_iota = lax.broadcasted_iota(jnp.int32, (slots, total), 0).astype(jnp.float32)
    picks, scaled_picks = [], []
    for j in range(line):
        hit = slot_iota == place[j : j + 1]
        picks.append(jnp.where(hit, 1.0, 0.0).astype(jnp.bfloat16))
        scaled_picks.append(jnp.where(hit, scales[j], 0.0).astype(jnp.bfloat16))

    for k in range(1, line):
        ones[k].wait_recv()
    gathered = rows1[...].reshape(total, 2 * dim)
    twos = {}
    order = far_first(line) + [0]
    half = max(1, line // 2)
    for start in range(0, line, half):
        group = order[start : start + half]
        tok_rows = dot_nn(jnp.concatenate([picks[j] for j in group], axis=0), gathered[:, 0:dim]).astype(jnp.bfloat16)
        grad_rows = dot_nn(jnp.concatenate([scaled_picks[j] for j in group], axis=0), gathered[:, dim:]).astype(
            jnp.bfloat16
        )
        for i, j in enumerate(group):
            there = send2 if j else recv2
            there[j, :, 0:dim] = tok_rows[i * slots : (i + 1) * slots]
            there[j, :, dim:] = grad_rows[i * slots : (i + 1) * slots]
            if j:
                twos[j] = remote(send2.at[j], recv2.at[j], two_s.at[j], two_r.at[j], on_b(j))
    pending += list(twos.values())

    for k in range(1, ring):
        weights[k].wait_recv()
    shared = remote(wbuf.at[:, c], wbuf.at[:, c], ws_s, ws_r, sibling)
    pending.append(shared)
    for j in range(1, line):
        twos[j].wait_recv()
    shared.wait_recv()

    in_rows = recv2[:, :, 0:dim].reshape(line * slots, dim)
    scaled = recv2[:, :, dim:].reshape(line * slots, dim)
    w_gate = wbuf[:, :, :, 0:hid].reshape(dim, hid)
    w_up = wbuf[:, :, :, hid : 2 * hid].reshape(dim, hid)
    w_down = wbuf[:, :, :, 2 * hid :].reshape(dim, hid)
    gate_pre = dot_nn(in_rows, w_gate)
    up_pre = dot_nn(in_rows, w_up)
    hid_grad = dot_nn(scaled, w_down)
    sig = jax.nn.sigmoid(gate_pre)
    act = gate_pre * sig
    hidden = (act * up_pre).astype(jnp.bfloat16)
    score = jnp.sum(hidden.astype(jnp.float32) * hid_grad, axis=1, keepdims=True)
    gate_grad = (hid_grad * up_pre * sig * (1.0 + gate_pre * (1.0 - sig))).astype(jnp.bfloat16)
    up_grad = (hid_grad * act).astype(jnp.bfloat16)

    in_grad = (dot_nt(gate_grad, w_gate) + dot_nt(up_grad, w_up)).astype(jnp.bfloat16)
    lane = lax.broadcasted_iota(jnp.int32, (line * slots, LANES), 1)
    score_lanes = jnp.where(lane == expert, score, 0.0).astype(jnp.bfloat16)
    backs = {}
    for j in order:
        there = back_out if j else back_in
        there[j, :, 0:dim] = in_grad[j * slots : (j + 1) * slots]
        there[j, :, dim:] = score_lanes[j * slots : (j + 1) * slots]
        if j:
            backs[j] = remote(back_out.at[j], back_in.at[j], back_s.at[j], back_r.at[j], on_b(-j))
    pending += list(backs.values())

    ahead, behind = ring // 2, ring - 1 - ring // 2
    targets = sorted(range(-behind, ahead + 1), key=lambda k: (-abs(k), -k))
    pair_grad = jnp.concatenate([gate_grad, up_grad], axis=1)
    sibs = {}
    for i, k in enumerate(targets):
        zt = (z + k + ring) % ring
        cut = pl.ds(pl.multiple_of(zt * (2 * shard), 2 * shard), 2 * shard)
        cut_grad = pl.ds(pl.multiple_of(dim + zt * (2 * shard), 2 * shard), 2 * shard)
        cols_in = recv2[:, :, cut].reshape(line * slots, 2 * shard)
        cols_scaled = recv2[:, :, cut_grad].reshape(line * slots, 2 * shard)
        part[i, :, :, 0 : 2 * hid] = dot_tn(cols_in, pair_grad).astype(jnp.bfloat16).reshape(2, shard, 2 * hid)
        part[i, :, :, 2 * hid :] = dot_tn(cols_scaled, hidden).astype(jnp.bfloat16).reshape(2, shard, hid)
        sibs[k] = remote(part.at[i, 1 - c], sib.at[i], sib_s.at[i], sib_r.at[i], sibling)
    pending += list(sibs.values())

    def chip_sum(k):
        i = targets.index(k)
        sibs[k].wait_recv()
        return part[i, c].astype(jnp.float32) + sib[i].astype(jnp.float32)

    pluses, minuses = {}, {}

    def hop_plus(h):
        value = chip_sum(ahead - h)
        if h:
            pluses[h - 1].wait_recv()
            value = value + plus_in[h - 1].astype(jnp.float32)
        plus_out[h] = value.astype(jnp.bfloat16)
        pluses[h] = remote(plus_out.at[h], plus_in.at[h], plus_s.at[h], plus_r.at[h], on_z(1))

    def hop_minus(h):
        value = chip_sum(h - behind)
        if h:
            minuses[h - 1].wait_recv()
            value = value + minus_in[h - 1].astype(jnp.float32)
        minus_out[h] = value.astype(jnp.bfloat16)
        minuses[h] = remote(minus_out.at[h], minus_in.at[h], minus_s.at[h], minus_r.at[h], on_z(-1))

    homes = {}

    def combine():
        for j in range(1, line):
            backs[j].wait_recv()
        pick = jnp.concatenate(picks, axis=0)
        summed = dot_tn(pick, back_in[...].reshape(line * slots, dim + LANES)).astype(jnp.bfloat16)
        for p in far_first(line) + [0]:
            there = home_out if p else home_in
            there[p] = summed[p * tok : (p + 1) * tok]
            if p:
                homes[p] = remote(home_out.at[p], home_in.at[p], home_s.at[p], home_r.at[p], on_a(-p))

    for h in range(ahead):
        if h == ahead // 2:
            combine()
        hop_plus(h)
        if h < behind:
            hop_minus(h)
    pending += list(homes.values()) + list(pluses.values()) + list(minuses.values())

    for p in range(1, line):
        homes[p].wait_recv()
    back = home_in[0].astype(jnp.float32)
    for p in range(1, line):
        back = back + home_in[p].astype(jnp.float32)
    dtok_ref[...] = back[:, 0:dim].astype(jnp.bfloat16)
    eye = (
        lax.broadcasted_iota(jnp.int32, (LANES, LANES), 0) == lax.broadcasted_iota(jnp.int32, (LANES, LANES), 1)
    ).astype(jnp.float32).astype(jnp.bfloat16)
    by_expert = dot_nt(eye, back[:, dim:].astype(jnp.bfloat16))
    expert_iota = lax.broadcasted_iota(jnp.int32, (LANES, tok), 0)
    chosen = [
        jnp.sum(jnp.where(expert_iota == ids_ref[k : k + 1, :], by_expert, 0.0), axis=0, keepdims=True)
        for k in range(top)
    ]
    dgate_ref[...] = (jnp.concatenate(chosen, axis=0) / gates_f).astype(jnp.bfloat16)

    summed = chip_sum(0)
    pluses[ahead - 1].wait_recv()
    summed = summed + plus_in[ahead - 1].astype(jnp.float32)
    if behind:
        minuses[behind - 1].wait_recv()
        summed = summed + minus_in[behind - 1].astype(jnp.float32)
    dwg_ref[...] = summed[:, 0:hid]
    dwu_ref[...] = summed[:, hid : 2 * hid]
    dwd_ref[...] = summed[:, 2 * hid :]

    for copy in pending:
        copy.wait_send()


def per_device(line, ring, cap, tokens, out_grad, expert_ids, gates, w_gate, w_up, w_down):
    tok, dim = tokens.shape
    top = expert_ids.shape[1]
    _, shard, hid = w_gate.shape
    slots = line * cap
    ahead, behind = ring // 2, ring - 1 - ring // 2
    bf16, f32 = jnp.bfloat16, jnp.float32
    dma = pltpu.SemaphoreType.DMA
    vmem = pl.BlockSpec(memory_space=pltpu.VMEM)
    d_tokens, d_gates, d_gate_w, d_up_w, d_down_w = pl.pallas_call(
        functools.partial(kernel, line, ring, cap),
        out_shape=[
            jax.ShapeDtypeStruct((tok, dim), bf16),
            jax.ShapeDtypeStruct((top, tok), bf16),
            jax.ShapeDtypeStruct((shard, hid), f32),
            jax.ShapeDtypeStruct((shard, hid), f32),
            jax.ShapeDtypeStruct((shard, hid), f32),
        ],
        in_specs=[vmem] * 7,
        out_specs=[vmem] * 5,
        scratch_shapes=[
            pltpu.VMEM((line, 2 * top, LANES), bf16),
            pltpu.VMEM((line, tok, 2 * dim), bf16),
            pltpu.VMEM((line, slots, 2 * dim), bf16),
            pltpu.VMEM((line, slots, 2 * dim), bf16),
            pltpu.VMEM((ring, 2, shard, 3 * hid), bf16),
            pltpu.VMEM((line, slots, dim + LANES), bf16),
            pltpu.VMEM((line, slots, dim + LANES), bf16),
            pltpu.VMEM((line, tok, dim + LANES), bf16),
            pltpu.VMEM((line, tok, dim + LANES), bf16),
            pltpu.VMEM((ring, 2, shard, 3 * hid), bf16),
            pltpu.VMEM((ring, shard, 3 * hid), bf16),
            pltpu.VMEM((ahead, shard, 3 * hid), bf16),
            pltpu.VMEM((ahead, shard, 3 * hid), bf16),
            pltpu.VMEM((max(behind, 1), shard, 3 * hid), bf16),
            pltpu.VMEM((max(behind, 1), shard, 3 * hid), bf16),
            dma((line,)), dma((line,)), dma((line,)), dma((line,)), dma((line,)), dma((line,)),
            dma((ring,)), dma((ring,)), dma(()), dma(()),
            dma((line,)), dma((line,)), dma((line,)), dma((line,)),
            dma((ring,)), dma((ring,)),
            dma((ahead,)), dma((ahead,)), dma((max(behind, 1),)), dma((max(behind, 1),)),
        ],
        compiler_params=pltpu.CompilerParams(
            collective_id=0, has_side_effects=True, vmem_limit_bytes=56 * 1024 * 1024
        ),
        name="expert_backward",
    )(tokens, out_grad, expert_ids.T, gates.T, w_gate[0], w_up[0], w_down[0])
    return d_tokens, d_gates.T, d_gate_w[None], d_up_w[None], d_down_w[None]


def solution(mesh, cap=6):
    experts, groups = mesh.shape["expert"], mesh.shape["dp"]
    line = 1
    while line * line < experts:
        line += 1
    split, both = P("expert", "dp", None), P(("expert", "dp"), None)
    return jax.shard_map(
        functools.partial(per_device, line, groups // 2, cap),
        mesh=mesh,
        in_specs=(both, both, both, both, split, split, split),
        out_specs=(both, both, split, split, split),
        check_vma=False,
    )
```

```python
import functools

import jax
import jax.numpy as jnp
from jax import lax
from jax.experimental import pallas as pl
from jax.experimental.pallas import tpu as pltpu
from jax.sharding import PartitionSpec as P

MESH = pl.DeviceIdType.MESH
LANES = 128


def dot_nn(a, b):
    return lax.dot_general(a, b, (((1,), (0,)), ((), ())), preferred_element_type=jnp.float32)


def dot_nt(a, b):
    return lax.dot_general(a, b, (((1,), (1,)), ((), ())), preferred_element_type=jnp.float32)


def dot_tn(a, b):
    return lax.dot_general(a, b, (((0,), (0,)), ((), ())), preferred_element_type=jnp.float32)


def split_rows(slots):
    return (0, 16), (16, slots)


def kernel(
    line, ring, cap,
    tok_ref, grad_ref, ids_ref, gates_ref, wg_ref, wu_ref, wd_ref,
    dtok_ref, dgate_ref, dwg_ref, dwu_ref, dwd_ref,
    meta, rows1, send2, recv2, wbuf, acts, back_out, back_in, home_out, home_in,
    part, sib, plus_out, plus_in, minus_out, minus_in,
    meta_s, meta_r, one_s, one_r, two_s, two_r, w_s, w_r, ws_s, ws_r,
    back_s, back_r, home_s, home_r, sib_s, sib_r, plus_s, plus_r, minus_s, minus_r,
):
    tok, dim = tok_ref.shape
    top = ids_ref.shape[0]
    hid = wg_ref.shape[1]
    slots = line * cap
    shard = wg_ref.shape[0]
    parts = split_rows(slots)
    offsets = sorted(range(line), key=lambda k: (min(k, line - k), k))
    place_of = {k: q for q, k in enumerate(offsets)}

    expert = lax.axis_index("expert")
    dp = lax.axis_index("dp")
    z, c = dp // 2, dp % 2
    stride_a = line - (line - 1) * c
    stride_b = 1 + (line - 1) * c
    y, x = expert // line, expert % line
    a = y * (1 - c) + x * c
    b = x * (1 - c) + y * c

    def on_a(k):
        return (((a + k + line) % line) * stride_a + b * stride_b, dp)

    def on_b(k):
        return (a * stride_a + ((b + k + line) % line) * stride_b, dp)

    def z_at(k):
        return (z + k + ring) % ring

    def on_z(k):
        return (expert, z_at(k) * 2 + c)

    sibling = (expert, z * 2 + 1 - c)
    pending = []

    def remote(src, dst, send, recv, target):
        copy = pltpu.make_async_remote_copy(
            src_ref=src, dst_ref=dst, send_sem=send, recv_sem=recv, device_id=target, device_id_type=MESH
        )
        copy.start()
        pending.append(copy)
        return copy

    barrier = pltpu.get_barrier_semaphore()
    for k in range(1, line):
        pl.semaphore_signal(barrier, inc=1, device_id=on_a(k), device_id_type=MESH)
        pl.semaphore_signal(barrier, inc=1, device_id=on_b(k), device_id_type=MESH)
    for k in range(1, ring):
        pl.semaphore_signal(barrier, inc=1, device_id=on_z(k), device_id_type=MESH)
    pl.semaphore_signal(barrier, inc=1, device_id=sibling, device_id_type=MESH)

    ids_f = ids_ref[...].astype(jnp.float32)
    gates_f = gates_ref[...].astype(jnp.float32)
    meta[0, :, 0:tok] = jnp.concatenate([ids_f, gates_f], axis=0).astype(jnp.bfloat16)
    meta[0, :, tok:] = jnp.zeros((2 * top, LANES - tok), jnp.bfloat16)
    rows1[0, :, 0:dim] = tok_ref[...]
    rows1[0, :, dim:] = grad_ref[...]
    wbuf[z, c, :, 0:hid] = wg_ref[...]
    wbuf[z, c, :, hid : 2 * hid] = wu_ref[...]
    wbuf[z, c, :, 2 * hid :] = wd_ref[...]

    pl.semaphore_wait(barrier, 2 * (line - 1) + ring)

    metas, ones, weights, shared = {}, {}, {}, {}
    for q in range(1, line):
        metas[q] = remote(meta.at[0], meta.at[q], meta_s.at[q], meta_r.at[q], on_a(offsets[q]))

    def send_rows(q, source, target, i=0, lanes=(0, 2 * dim)):
        cut = slice(*lanes)
        ones[q, i] = remote(
            rows1.at[source, :, cut], rows1.at[q, :, cut], one_s.at[q, i], one_r.at[q, i], on_a(target)
        )

    def send_weights(key, k, target, rows=(0, shard)):
        i, cut = len(weights), slice(*rows)
        ref = wbuf.at[z_at(-k), c, cut]
        weights[key] = remote(ref, ref, w_s.at[i], w_r.at[i], on_z(target))

    def share(k):
        i = len(shared)
        ref = wbuf.at[z_at(-k), c]
        shared[k] = remote(ref, ref, ws_s.at[i], ws_r.at[i], sibling)

    near = (1, -1, 2, -2)
    for k in near:
        send_rows(place_of[k % line], 0, k)
    for k in near:
        send_weights(k, 0, k)
    share(0)

    for q in range(1, line):
        metas[q].wait_recv()
    every = jnp.concatenate([meta[q].astype(jnp.float32)[:, 0:tok] for q in range(line)], axis=1)
    ids_all, gates_all = every[0:top], every[top:]
    total = line * tok
    masks, scales = [], []
    for j in range(line):
        named = (a * stride_a + ((b + j) % line) * stride_b).astype(jnp.float32)
        hit = ids_all == named
        masks.append(jnp.sum(jnp.where(hit, 1.0, 0.0), axis=0, keepdims=True))
        scales.append(jnp.sum(jnp.where(hit, gates_all, 0.0), axis=0, keepdims=True))
    mask = jnp.concatenate(masks, axis=0)
    rows = lax.broadcasted_iota(jnp.int32, (total, total), 0)
    cols = lax.broadcasted_iota(jnp.int32, (total, total), 1)
    earlier = ((rows < cols) & (rows // tok == cols // tok)).astype(jnp.float32).astype(jnp.bfloat16)
    pos = dot_nn(mask.astype(jnp.bfloat16), earlier)
    first = (lax.broadcasted_iota(jnp.int32, (line, total), 1) // tok * cap).astype(jnp.float32)
    place = jnp.where(mask > 0.0, first + pos, -1.0)
    holds = [(lo // cap, -(-hi // cap)) for lo, hi in parts]
    slot_iota = lax.broadcasted_iota(jnp.int32, (slots, total), 0).astype(jnp.float32)
    picks, scaled_picks = [[], []], [[], []]
    for j in range(line):
        hit = slot_iota == place[j : j + 1]
        pick = jnp.where(hit, 1.0, 0.0)
        scaled_pick = jnp.where(hit, scales[j], 0.0)
        for g, (lo, hi) in enumerate(parts):
            lanes = slice(holds[g][0] * tok, holds[g][1] * tok)
            picks[g].append(pick[lo:hi, lanes].astype(jnp.bfloat16))
            scaled_picks[g].append(scaled_pick[lo:hi, lanes].astype(jnp.bfloat16))
    picks = [jnp.concatenate(p, axis=0) for p in picks]
    scaled_picks = [jnp.concatenate(p, axis=0) for p in scaled_picks]

    twos = {}

    def dispatch(g):
        (lo, hi), (q0, q1) = parts[g], holds[g]
        count = hi - lo
        for col, pick in ((0, picks[g]), (dim, scaled_picks[g])):
            held = rows1[q0:q1, :, col : col + dim].reshape((q1 - q0) * tok, dim)
            out = dot_nn(pick, held).astype(jnp.bfloat16)
            for j in range(line):
                (send2 if j else recv2)[j, lo:hi, col : col + dim] = out[j * count : (j + 1) * count]
        for q in range(1, line):
            j = offsets[q]
            twos[j, g] = remote(
                send2.at[j, lo:hi], recv2.at[j, lo:hi], two_s.at[j, g], two_r.at[j, g], on_b(j)
            )

    for k in (1, -1):
        ones[place_of[k % line], 0].wait_recv()
    dispatch(0)
    for k in (2, -2):
        ones[place_of[k % line], 0].wait_recv()
    send_rows(place_of[3], place_of[2], 1)
    send_rows(place_of[-3 % line], place_of[-2 % line], -1)
    send_rows(place_of[4], place_of[2], 2, 0, (0, dim))
    send_rows(place_of[4], place_of[-2 % line], -2, 1, (dim, 2 * dim))
    for q, i in ((place_of[3], 0), (place_of[-3 % line], 0), (place_of[4], 0), (place_of[4], 1)):
        ones[q, i].wait_recv()
    dispatch(1)

    for k in near:
        weights[k].wait_recv()
    send_weights(3, 2, 1)
    send_weights(-3, -2, -1)
    send_weights(4, 2, 2, (0, shard // 2))
    send_weights(-4, -2, -2, (shard // 2, shard))
    for k in near:
        share(k)
    for k in (3, -3, 4, -4):
        weights[k].wait_recv()
    for k in (3, -3, 4):
        share(k)
    for copy in list(shared.values()):
        copy.wait_recv()

    backs = {}

    def expert_rows(g):
        lo, hi = parts[g]
        count = hi - lo
        in_rows = recv2[:, lo:hi, 0:dim].reshape(line * count, dim)
        scaled = recv2[:, lo:hi, dim:].reshape(line * count, dim)
        w_pair = wbuf[:, :, :, 0 : 2 * hid].reshape(dim, 2 * hid)
        w_down = wbuf[:, :, :, 2 * hid :].reshape(dim, hid)
        pre = dot_nn(in_rows, w_pair)
        gate_pre, up_pre = pre[:, 0:hid], pre[:, hid:]
        hid_grad = dot_nn(scaled, w_down)
        sig = jax.nn.sigmoid(gate_pre)
        act = gate_pre * sig
        hidden = (act * up_pre).astype(jnp.bfloat16)
        score = jnp.sum(hidden.astype(jnp.float32) * hid_grad, axis=1, keepdims=True)
        gate_grad = (hid_grad * up_pre * sig * (1.0 + gate_pre * (1.0 - sig))).astype(jnp.bfloat16)
        up_grad = (hid_grad * act).astype(jnp.bfloat16)
        pair = jnp.concatenate([gate_grad, up_grad], axis=1)
        acts[:, lo:hi, 0 : 2 * hid] = pair.reshape(line, count, 2 * hid)
        acts[:, lo:hi, 2 * hid :] = hidden.reshape(line, count, hid)
        in_grad = dot_nt(pair, w_pair).astype(jnp.bfloat16)
        lane = lax.broadcasted_iota(jnp.int32, (line * count, LANES), 1)
        score_lanes = jnp.where(lane == expert, score, 0.0).astype(jnp.bfloat16)
        for j in offsets:
            there = back_out if j else back_in
            there[j, lo:hi, 0:dim] = in_grad[j * count : (j + 1) * count]
            there[j, lo:hi, dim:] = score_lanes[j * count : (j + 1) * count]
        for j in offsets[1:]:
            backs[j, g] = remote(
                back_out.at[j, lo:hi], back_in.at[j, lo:hi], back_s.at[j, g], back_r.at[j, g], on_b(-j)
            )

    for j in range(1, line):
        twos[j, 0].wait_recv()
    expert_rows(0)
    for j in range(1, line):
        twos[j, 1].wait_recv()
    expert_rows(1)

    ahead, behind = ring // 2, ring - 1 - ring // 2
    targets = sorted(range(-behind, ahead + 1), key=lambda k: (-abs(k), -k))
    pair_grad = acts[:, :, 0 : 2 * hid].reshape(line * slots, 2 * hid)
    hidden = acts[:, :, 2 * hid :].reshape(line * slots, hid)
    sibs = {}
    for i, k in enumerate(targets):
        zt = z_at(k)
        cut = pl.ds(pl.multiple_of(zt * (2 * shard), 2 * shard), 2 * shard)
        cut_grad = pl.ds(pl.multiple_of(dim + zt * (2 * shard), 2 * shard), 2 * shard)
        cols_in = recv2[:, :, cut].reshape(line * slots, 2 * shard)
        cols_scaled = recv2[:, :, cut_grad].reshape(line * slots, 2 * shard)
        part[i, :, :, 0 : 2 * hid] = dot_tn(cols_in, pair_grad).astype(jnp.bfloat16).reshape(2, shard, 2 * hid)
        part[i, :, :, 2 * hid :] = dot_tn(cols_scaled, hidden).astype(jnp.bfloat16).reshape(2, shard, hid)
        sibs[k] = remote(part.at[i, 1 - c], sib.at[i], sib_s.at[i], sib_r.at[i], sibling)

    met = set()

    def chip_sum(k, m):
        i, lanes = targets.index(k), slice(m * hid, (m + 1) * hid)
        if k not in met:
            sibs[k].wait_recv()
            met.add(k)
        return part[i, c, :, lanes].astype(jnp.float32) + sib[i, :, lanes].astype(jnp.float32)

    pluses, minuses = {}, {}

    def hop(h, m, k, done, out, inn, send, recv, way):
        value = chip_sum(k, m)
        if h:
            done[h - 1, m].wait_recv()
            value = value + inn[h - 1, m].astype(jnp.float32)
        out[h, m] = value.astype(jnp.bfloat16)
        done[h, m] = remote(out.at[h, m], inn.at[h, m], send.at[h, m], recv.at[h, m], on_z(way))

    def hops(h):
        for m in range(3):
            hop(h, m, ahead - h, pluses, plus_out, plus_in, plus_s, plus_r, 1)
            if h < behind:
                hop(h, m, h - behind, minuses, minus_out, minus_in, minus_s, minus_r, -1)

    homes = {}

    def send_home(q, block):
        (home_out if q else home_in)[q] = block.astype(jnp.bfloat16)
        if q:
            homes[q] = remote(home_out.at[q], home_in.at[q], home_s.at[q], home_r.at[q], on_a(-offsets[q]))

    def combine(g):
        lo, hi = parts[g]
        for j in range(1, line):
            backs[j, g].wait_recv()
        return dot_tn(picks[g], back_in[:, lo:hi].reshape(line * (hi - lo), dim + LANES))

    hops(0)
    early = combine(0)
    for q in range(holds[1][0]):
        send_home(q, early[q * tok : (q + 1) * tok])
    early = early[holds[1][0] * tok :]
    hops(1)
    late = combine(1)
    for q in list(range(holds[1][0] + 1, line)) + [holds[1][0]]:
        i = q - holds[1][0]
        block = late[i * tok : (i + 1) * tok]
        if q < holds[0][1]:
            block = block + early[i * tok : (i + 1) * tok]
        send_home(q, block)
    for h in range(2, ahead):
        hops(h)

    for q in range(1, line):
        homes[q].wait_recv()
    back = home_in[0].astype(jnp.float32)
    for q in range(1, line):
        back = back + home_in[q].astype(jnp.float32)
    dtok_ref[...] = back[:, 0:dim].astype(jnp.bfloat16)
    eye = (
        lax.broadcasted_iota(jnp.int32, (LANES, LANES), 0) == lax.broadcasted_iota(jnp.int32, (LANES, LANES), 1)
    ).astype(jnp.float32).astype(jnp.bfloat16)
    by_expert = dot_nt(eye, back[:, dim:].astype(jnp.bfloat16))
    expert_iota = lax.broadcasted_iota(jnp.int32, (LANES, tok), 0)
    chosen = [
        jnp.sum(jnp.where(expert_iota == ids_ref[k : k + 1, :], by_expert, 0.0), axis=0, keepdims=True)
        for k in range(top)
    ]
    dgate_ref[...] = (jnp.concatenate(chosen, axis=0) / gates_f).astype(jnp.bfloat16)

    for m, out_ref in enumerate((dwg_ref, dwu_ref, dwd_ref)):
        pluses[ahead - 1, m].wait_recv()
        minuses[behind - 1, m].wait_recv()
        out_ref[...] = (
            chip_sum(0, m) + plus_in[ahead - 1, m].astype(jnp.float32) + minus_in[behind - 1, m].astype(jnp.float32)
        )

    for copy in pending:
        copy.wait_send()


def hand_on(*refs):
    half = len(refs) // 2
    for source, target in zip(refs[:half], refs[half:]):
        target[...] = source[...]


def per_device(line, ring, cap, tokens, out_grad, expert_ids, gates, w_gate, w_up, w_down):
    tok, dim = tokens.shape
    top = expert_ids.shape[1]
    _, shard, hid = w_gate.shape
    slots = line * cap
    ahead, behind = ring // 2, ring - 1 - ring // 2
    bf16, f32 = jnp.bfloat16, jnp.float32
    dma = pltpu.SemaphoreType.DMA
    vmem = pl.BlockSpec(memory_space=pltpu.VMEM)
    shapes = [
        jax.ShapeDtypeStruct((tok, dim), bf16),
        jax.ShapeDtypeStruct((top, tok), bf16),
        jax.ShapeDtypeStruct((shard, hid), f32),
        jax.ShapeDtypeStruct((shard, hid), f32),
        jax.ShapeDtypeStruct((shard, hid), f32),
    ]
    results = pl.pallas_call(
        functools.partial(kernel, line, ring, cap),
        out_shape=shapes,
        in_specs=[vmem] * 7,
        out_specs=[vmem] * 5,
        scratch_shapes=[
            pltpu.VMEM((line, 2 * top, LANES), bf16),
            pltpu.VMEM((line, tok, 2 * dim), bf16),
            pltpu.VMEM((line, slots, 2 * dim), bf16),
            pltpu.VMEM((line, slots, 2 * dim), bf16),
            pltpu.VMEM((ring, 2, shard, 3 * hid), bf16),
            pltpu.VMEM((line, slots, 3 * hid), bf16),
            pltpu.VMEM((line, slots, dim + LANES), bf16),
            pltpu.VMEM((line, slots, dim + LANES), bf16),
            pltpu.VMEM((line, tok, dim + LANES), bf16),
            pltpu.VMEM((line, tok, dim + LANES), bf16),
            pltpu.VMEM((ring, 2, shard, 3 * hid), bf16),
            pltpu.VMEM((ring, shard, 3 * hid), bf16),
            pltpu.VMEM((ahead, 3, shard, hid), bf16),
            pltpu.VMEM((ahead, 3, shard, hid), bf16),
            pltpu.VMEM((behind, 3, shard, hid), bf16),
            pltpu.VMEM((behind, 3, shard, hid), bf16),
            dma((line,)), dma((line,)), dma((line, 2)), dma((line, 2)), dma((line, 2)), dma((line, 2)),
            dma((ring,)), dma((ring,)), dma((ring,)), dma((ring,)),
            dma((line, 2)), dma((line, 2)), dma((line,)), dma((line,)),
            dma((ring,)), dma((ring,)),
            dma((ahead, 3)), dma((ahead, 3)), dma((behind, 3)), dma((behind, 3)),
        ],
        compiler_params=pltpu.CompilerParams(
            collective_id=0, has_side_effects=True, vmem_limit_bytes=56 * 1024 * 1024
        ),
        name="expert_backward",
    )(tokens, out_grad, expert_ids.T, gates.T, w_gate[0], w_up[0], w_down[0])
    d_tokens, d_gates, d_gate_w, d_up_w, d_down_w = pl.pallas_call(
        hand_on, out_shape=shapes, in_specs=[vmem] * 5, out_specs=[vmem] * 5, name="hand_on"
    )(*results)
    return d_tokens, d_gates.T, d_gate_w[None], d_up_w[None], d_down_w[None]


def solution(mesh):
    experts, groups = mesh.shape["expert"], mesh.shape["dp"]
    line = 1
    while line * line < experts:
        line += 1
    split, both = P("expert", "dp", None), P(("expert", "dp"), None)

    def whole(tokens, out_grad, expert_ids, gates, w_gate, w_up, w_down):
        tok = tokens.shape[0] // (experts * groups)
        cap = max(2, 3 * tok * expert_ids.shape[1] // (2 * experts))
        return jax.shard_map(
            functools.partial(per_device, line, groups // 2, cap),
            mesh=mesh,
            in_specs=(both, both, both, both, split, split, split),
            out_specs=(both, both, split, split, split),
            check_vma=False,
        )(tokens, out_grad, expert_ids, gates, w_gate, w_up, w_down)

    return whole
```

```python
import functools

import jax
import jax.numpy as jnp
from jax import lax
from jax.experimental import pallas as pl
from jax.experimental.pallas import tpu as pltpu
from jax.sharding import PartitionSpec as P

MESH = pl.DeviceIdType.MESH
LANES = 128


def dot_nn(a, b):
    return lax.dot_general(a, b, (((1,), (0,)), ((), ())), preferred_element_type=jnp.float32)


def dot_nt(a, b):
    return lax.dot_general(a, b, (((1,), (1,)), ((), ())), preferred_element_type=jnp.float32)


def dot_tn(a, b):
    return lax.dot_general(a, b, (((0,), (0,)), ((), ())), preferred_element_type=jnp.float32)


def split_rows(slots):
    return [(lo, lo + 16) for lo in range(0, slots, 16)]


def kernel(
    line, ring, cap,
    tok_ref, grad_ref, ids_ref, gates_ref, wg_ref, wu_ref, wd_ref,
    dtok_ref, dgate_ref, dwg_ref, dwu_ref, dwd_ref,
    meta, rows1, send2, recv2, wbuf, acts, back_out, back_in, home_out, home_in,
    part, sib, plus_out, plus_in, minus_out, minus_in,
    meta_s, meta_r, one_s, one_r, two_s, two_r, w_s, w_r, ws_s, ws_r,
    back_s, back_r, home_s, home_r, sib_s, sib_r, plus_s, plus_r, minus_s, minus_r,
):
    tok, dim = tok_ref.shape
    top = ids_ref.shape[0]
    hid = wg_ref.shape[1]
    slots = line * cap
    shard = wg_ref.shape[0]
    parts = split_rows(slots)
    offsets = sorted(range(line), key=lambda k: (min(k, line - k), k))
    place_of = {k: q for q, k in enumerate(offsets)}

    expert = lax.axis_index("expert")
    dp = lax.axis_index("dp")
    z, c = dp // 2, dp % 2
    stride_a = line - (line - 1) * c
    stride_b = 1 + (line - 1) * c
    y, x = expert // line, expert % line
    a = y * (1 - c) + x * c
    b = x * (1 - c) + y * c

    def on_a(k):
        return (((a + k + line) % line) * stride_a + b * stride_b, dp)

    def on_b(k):
        return (a * stride_a + ((b + k + line) % line) * stride_b, dp)

    def z_at(k):
        return (z + k + ring) % ring

    def on_z(k):
        return (expert, z_at(k) * 2 + c)

    sibling = (expert, z * 2 + 1 - c)
    pending = []

    def remote(src, dst, send, recv, target):
        copy = pltpu.make_async_remote_copy(
            src_ref=src, dst_ref=dst, send_sem=send, recv_sem=recv, device_id=target, device_id_type=MESH
        )
        copy.start()
        pending.append(copy)
        return copy

    barrier = pltpu.get_barrier_semaphore()
    for k in range(1, line):
        pl.semaphore_signal(barrier, inc=1, device_id=on_a(k), device_id_type=MESH)
        pl.semaphore_signal(barrier, inc=1, device_id=on_b(k), device_id_type=MESH)
    for k in range(1, ring):
        pl.semaphore_signal(barrier, inc=1, device_id=on_z(k), device_id_type=MESH)
    pl.semaphore_signal(barrier, inc=1, device_id=sibling, device_id_type=MESH)

    ids_f = ids_ref[...].astype(jnp.float32)
    gates_f = gates_ref[...].astype(jnp.float32)
    meta[0, :, 0:tok] = jnp.concatenate([ids_f, gates_f], axis=0).astype(jnp.bfloat16)
    meta[0, :, tok:] = jnp.zeros((2 * top, LANES - tok), jnp.bfloat16)
    rows1[0, :, 0:dim] = tok_ref[...]
    rows1[0, :, dim:] = grad_ref[...]
    wbuf[z, c, :, 0:hid] = wg_ref[...]
    wbuf[z, c, :, hid : 2 * hid] = wu_ref[...]
    wbuf[z, c, :, 2 * hid :] = wd_ref[...]

    pl.semaphore_wait(barrier, 2 * (line - 1) + ring)

    metas, ones, weights, shared = {}, {}, {}, {}
    for q in range(1, line):
        metas[q] = remote(meta.at[0], meta.at[q], meta_s.at[q], meta_r.at[q], on_a(offsets[q]))

    def send_rows(q, source, target, i=0, lanes=(0, 2 * dim)):
        cut = slice(*lanes)
        ones[q, i] = remote(
            rows1.at[source, :, cut], rows1.at[q, :, cut], one_s.at[q, i], one_r.at[q, i], on_a(target)
        )

    def send_weights(key, k, target, rows=(0, shard)):
        i, cut = len(weights), slice(*rows)
        ref = wbuf.at[z_at(-k), c, cut]
        weights[key] = remote(ref, ref, w_s.at[i], w_r.at[i], on_z(target))

    def share(k):
        i = len(shared)
        ref = wbuf.at[z_at(-k), c]
        shared[k] = remote(ref, ref, ws_s.at[i], ws_r.at[i], sibling)

    near = (1, -1, 2, -2)
    halves = ((0, 2 * dim),)
    for i, lanes in enumerate(halves):
        for k in near:
            send_rows(place_of[k % line], 0, k, i, lanes)
    for k in near:
        send_weights(k, 0, k)
    share(0)

    for q in range(1, line):
        metas[q].wait_recv()
    every = jnp.concatenate([meta[q].astype(jnp.float32)[:, 0:tok] for q in range(line)], axis=1)
    ids_all, gates_all = every[0:top], every[top:]
    total = line * tok
    masks, scales = [], []
    for j in range(line):
        named = (a * stride_a + ((b + j) % line) * stride_b).astype(jnp.float32)
        hit = ids_all == named
        masks.append(jnp.sum(jnp.where(hit, 1.0, 0.0), axis=0, keepdims=True))
        scales.append(jnp.sum(jnp.where(hit, gates_all, 0.0), axis=0, keepdims=True))
    mask = jnp.concatenate(masks, axis=0)
    rows = lax.broadcasted_iota(jnp.int32, (total, total), 0)
    cols = lax.broadcasted_iota(jnp.int32, (total, total), 1)
    earlier = ((rows < cols) & (rows // tok == cols // tok)).astype(jnp.float32).astype(jnp.bfloat16)
    pos = dot_nn(mask.astype(jnp.bfloat16), earlier)
    first = (lax.broadcasted_iota(jnp.int32, (line, total), 1) // tok * cap).astype(jnp.float32)
    place = jnp.where(mask > 0.0, first + pos, -1.0)
    holds = [(lo // cap, -(-hi // cap)) for lo, hi in parts]
    slot_iota = lax.broadcasted_iota(jnp.int32, (slots, total), 0).astype(jnp.float32)
    picks, scaled_picks = [[] for _ in parts], [[] for _ in parts]
    for j in range(line):
        hit = slot_iota == place[j : j + 1]
        pick = jnp.where(hit, 1.0, 0.0)
        scaled_pick = jnp.where(hit, scales[j], 0.0)
        for g, (lo, hi) in enumerate(parts):
            lanes = slice(holds[g][0] * tok, holds[g][1] * tok)
            picks[g].append(pick[lo:hi, lanes].astype(jnp.bfloat16))
            scaled_picks[g].append(scaled_pick[lo:hi, lanes].astype(jnp.bfloat16))
    picks = [jnp.concatenate(p, axis=0) for p in picks]
    scaled_picks = [jnp.concatenate(p, axis=0) for p in scaled_picks]

    twos = {}

    def dispatch(g):
        (lo, hi), (q0, q1) = parts[g], holds[g]
        count = hi - lo
        for col, pick in ((0, picks[g]), (dim, scaled_picks[g])):
            held = rows1[q0:q1, :, col : col + dim].reshape((q1 - q0) * tok, dim)
            out = dot_nn(pick, held).astype(jnp.bfloat16)
            for j in range(line):
                (send2 if j else recv2)[j, lo:hi, col : col + dim] = out[j * count : (j + 1) * count]
        for j in offsets[1:]:
            twos[j, g] = remote(
                send2.at[j, lo:hi], recv2.at[j, lo:hi], two_s.at[j, g], two_r.at[j, g], on_b(j)
            )

    for i in range(len(halves)):
        for k in (1, -1):
            ones[place_of[k % line], i].wait_recv()
    dispatch(0)
    for i, lanes in enumerate(halves):
        for k in (2, -2):
            ones[place_of[k % line], i].wait_recv()
        send_rows(place_of[3], place_of[2], 1, i, lanes)
        send_rows(place_of[-3 % line], place_of[-2 % line], -1, i, lanes)
        if i == 0:
            send_rows(place_of[4], place_of[2], 2, 0, (0, dim))
        if i == len(halves) - 1:
            send_rows(place_of[4], place_of[-2 % line], -2, 1, (dim, 2 * dim))
    for i in range(len(halves)):
        for k in (3, -3):
            ones[place_of[k % line], i].wait_recv()
    dispatch(1)
    for i in range(2):
        ones[place_of[4], i].wait_recv()
    dispatch(2)

    for k in near:
        weights[k].wait_recv()
    send_weights(3, 2, 1)
    send_weights(-3, -2, -1)
    send_weights(4, 2, 2, (0, shard // 2))
    send_weights(-4, -2, -2, (shard // 2, shard))
    for k in near:
        share(k)
    for k in (3, -3, 4, -4):
        weights[k].wait_recv()
    for k in (3, -3, 4):
        share(k)
    for copy in list(shared.values()):
        copy.wait_recv()

    backs = {}

    def expert_rows(g):
        lo, hi = parts[g]
        count = hi - lo
        in_rows = recv2[:, lo:hi, 0:dim].reshape(line * count, dim)
        scaled = recv2[:, lo:hi, dim:].reshape(line * count, dim)
        w_pair = wbuf[:, :, :, 0 : 2 * hid].reshape(dim, 2 * hid)
        w_down = wbuf[:, :, :, 2 * hid :].reshape(dim, hid)
        pre = dot_nn(in_rows, w_pair)
        gate_pre, up_pre = pre[:, 0:hid], pre[:, hid:]
        hid_grad = dot_nn(scaled, w_down)
        sig = jax.nn.sigmoid(gate_pre)
        act = gate_pre * sig
        hidden = (act * up_pre).astype(jnp.bfloat16)
        score = jnp.sum(hidden.astype(jnp.float32) * hid_grad, axis=1, keepdims=True)
        gate_grad = (hid_grad * up_pre * sig * (1.0 + gate_pre * (1.0 - sig))).astype(jnp.bfloat16)
        up_grad = (hid_grad * act).astype(jnp.bfloat16)
        pair = jnp.concatenate([gate_grad, up_grad], axis=1)
        acts[:, lo:hi, 0 : 2 * hid] = pair.reshape(line, count, 2 * hid)
        acts[:, lo:hi, 2 * hid :] = hidden.reshape(line, count, hid)
        in_grad = dot_nt(pair, w_pair).astype(jnp.bfloat16)
        lane = lax.broadcasted_iota(jnp.int32, (line * count, LANES), 1)
        score_lanes = jnp.where(lane == expert, score, 0.0).astype(jnp.bfloat16)
        for j in offsets:
            there = back_out if j else back_in
            there[j, lo:hi, 0:dim] = in_grad[j * count : (j + 1) * count]
            there[j, lo:hi, dim:] = score_lanes[j * count : (j + 1) * count]
        for j in offsets[1:]:
            backs[j, g] = remote(
                back_out.at[j, lo:hi], back_in.at[j, lo:hi], back_s.at[j, g], back_r.at[j, g], on_b(-j)
            )

    for g in range(len(parts)):
        for j in range(1, line):
            twos[j, g].wait_recv()
        expert_rows(g)

    ahead, behind = ring // 2, ring - 1 - ring // 2
    targets = sorted(range(-behind, ahead + 1), key=lambda k: (-abs(k), -k))
    pair_grad = acts[:, :, 0 : 2 * hid].reshape(line * slots, 2 * hid)
    hidden = acts[:, :, 2 * hid :].reshape(line * slots, hid)
    sibs = {}
    for i, k in enumerate(targets):
        zt = z_at(k)
        cut = pl.ds(pl.multiple_of(zt * (2 * shard), 2 * shard), 2 * shard)
        cut_grad = pl.ds(pl.multiple_of(dim + zt * (2 * shard), 2 * shard), 2 * shard)
        cols_in = recv2[:, :, cut].reshape(line * slots, 2 * shard)
        cols_scaled = recv2[:, :, cut_grad].reshape(line * slots, 2 * shard)
        part[i, :, :, 0 : 2 * hid] = dot_tn(cols_in, pair_grad).astype(jnp.bfloat16).reshape(2, shard, 2 * hid)
        part[i, :, :, 2 * hid :] = dot_tn(cols_scaled, hidden).astype(jnp.bfloat16).reshape(2, shard, hid)
        sibs[k] = remote(part.at[i, 1 - c], sib.at[i], sib_s.at[i], sib_r.at[i], sibling)

    met = set()

    def chip_sum(k, m):
        i, lanes = targets.index(k), slice(m * hid, (m + 1) * hid)
        if k not in met:
            sibs[k].wait_recv()
            met.add(k)
        return part[i, c, :, lanes].astype(jnp.float32) + sib[i, :, lanes].astype(jnp.float32)

    pluses, minuses = {}, {}

    def hop(h, m, k, done, out, inn, send, recv, way):
        value = chip_sum(k, m)
        if h:
            done[h - 1, m].wait_recv()
            value = value + inn[h - 1, m].astype(jnp.float32)
        out[h, m] = value.astype(jnp.bfloat16)
        done[h, m] = remote(out.at[h, m], inn.at[h, m], send.at[h, m], recv.at[h, m], on_z(way))

    def hops(h):
        for m in range(3):
            hop(h, m, ahead - h, pluses, plus_out, plus_in, plus_s, plus_r, 1)
            if h < behind:
                hop(h, m, h - behind, minuses, minus_out, minus_in, minus_s, minus_r, -1)

    homes = {}

    def send_home(q, block):
        (home_out if q else home_in)[q] = block.astype(jnp.bfloat16)
        if q:
            homes[q] = remote(home_out.at[q], home_in.at[q], home_s.at[q], home_r.at[q], on_a(-offsets[q]))

    def combine(g):
        lo, hi = parts[g]
        for j in range(1, line):
            backs[j, g].wait_recv()
        return dot_tn(picks[g], back_in[:, lo:hi].reshape(line * (hi - lo), dim + LANES))

    rest = {}

    def settle(g):
        out, (q0, q1) = combine(g), holds[g]
        ready = holds[g + 1][0] if g + 1 < len(parts) else line
        for q in sorted(range(q0, q1), key=lambda q: -q):
            block = out[(q - q0) * tok : (q - q0 + 1) * tok]
            if q in rest:
                block = block + rest[q]
            if q < ready:
                send_home(q, block)
            else:
                rest[q] = block

    hops(0)
    settle(0)
    settle(1)
    hops(1)
    settle(2)
    for h in range(2, ahead):
        hops(h)

    for q in range(1, line):
        homes[q].wait_recv()
    back = home_in[0].astype(jnp.float32)
    for q in range(1, line):
        back = back + home_in[q].astype(jnp.float32)
    dtok_ref[...] = back[:, 0:dim].astype(jnp.bfloat16)
    eye = (
        lax.broadcasted_iota(jnp.int32, (LANES, LANES), 0) == lax.broadcasted_iota(jnp.int32, (LANES, LANES), 1)
    ).astype(jnp.float32).astype(jnp.bfloat16)
    by_expert = dot_nt(eye, back[:, dim:].astype(jnp.bfloat16))
    expert_iota = lax.broadcasted_iota(jnp.int32, (LANES, tok), 0)
    chosen = [
        jnp.sum(jnp.where(expert_iota == ids_ref[k : k + 1, :], by_expert, 0.0), axis=0, keepdims=True)
        for k in range(top)
    ]
    dgate_ref[...] = (jnp.concatenate(chosen, axis=0) / gates_f).astype(jnp.bfloat16)

    for m, out_ref in enumerate((dwg_ref, dwu_ref, dwd_ref)):
        pluses[ahead - 1, m].wait_recv()
        minuses[behind - 1, m].wait_recv()
        out_ref[...] = (
            chip_sum(0, m) + plus_in[ahead - 1, m].astype(jnp.float32) + minus_in[behind - 1, m].astype(jnp.float32)
        )

    for copy in pending:
        copy.wait_send()


def hand_on(*refs):
    half = len(refs) // 2
    for source, target in zip(refs[:half], refs[half:]):
        target[...] = source[...]


def per_device(line, ring, cap, tokens, out_grad, expert_ids, gates, w_gate, w_up, w_down):
    tok, dim = tokens.shape
    top = expert_ids.shape[1]
    _, shard, hid = w_gate.shape
    slots = line * cap
    ahead, behind = ring // 2, ring - 1 - ring // 2
    bf16, f32 = jnp.bfloat16, jnp.float32
    dma = pltpu.SemaphoreType.DMA
    vmem = pl.BlockSpec(memory_space=pltpu.VMEM)
    shapes = [
        jax.ShapeDtypeStruct((tok, dim), bf16),
        jax.ShapeDtypeStruct((top, tok), bf16),
        jax.ShapeDtypeStruct((shard, hid), f32),
        jax.ShapeDtypeStruct((shard, hid), f32),
        jax.ShapeDtypeStruct((shard, hid), f32),
    ]
    results = pl.pallas_call(
        functools.partial(kernel, line, ring, cap),
        out_shape=shapes,
        in_specs=[vmem] * 7,
        out_specs=[vmem] * 5,
        scratch_shapes=[
            pltpu.VMEM((line, 2 * top, LANES), bf16),
            pltpu.VMEM((line, tok, 2 * dim), bf16),
            pltpu.VMEM((line, slots, 2 * dim), bf16),
            pltpu.VMEM((line, slots, 2 * dim), bf16),
            pltpu.VMEM((ring, 2, shard, 3 * hid), bf16),
            pltpu.VMEM((line, slots, 3 * hid), bf16),
            pltpu.VMEM((line, slots, dim + LANES), bf16),
            pltpu.VMEM((line, slots, dim + LANES), bf16),
            pltpu.VMEM((line, tok, dim + LANES), bf16),
            pltpu.VMEM((line, tok, dim + LANES), bf16),
            pltpu.VMEM((ring, 2, shard, 3 * hid), bf16),
            pltpu.VMEM((ring, shard, 3 * hid), bf16),
            pltpu.VMEM((ahead, 3, shard, hid), bf16),
            pltpu.VMEM((ahead, 3, shard, hid), bf16),
            pltpu.VMEM((behind, 3, shard, hid), bf16),
            pltpu.VMEM((behind, 3, shard, hid), bf16),
            dma((line,)), dma((line,)), dma((line, 2)), dma((line, 2)), dma((line, 3)), dma((line, 3)),
            dma((ring,)), dma((ring,)), dma((ring,)), dma((ring,)),
            dma((line, 3)), dma((line, 3)), dma((line,)), dma((line,)),
            dma((ring,)), dma((ring,)),
            dma((ahead, 3)), dma((ahead, 3)), dma((behind, 3)), dma((behind, 3)),
        ],
        compiler_params=pltpu.CompilerParams(
            collective_id=0, has_side_effects=True, vmem_limit_bytes=56 * 1024 * 1024
        ),
        name="expert_backward",
    )(tokens, out_grad, expert_ids.T, gates.T, w_gate[0], w_up[0], w_down[0])
    d_tokens, d_gates, d_gate_w, d_up_w, d_down_w = pl.pallas_call(
        hand_on, out_shape=shapes, in_specs=[vmem] * 5, out_specs=[vmem] * 5, name="hand_on"
    )(*results)
    return d_tokens, d_gates.T, d_gate_w[None], d_up_w[None], d_down_w[None]


def solution(mesh):
    experts, groups = mesh.shape["expert"], mesh.shape["dp"]
    line = 1
    while line * line < experts:
        line += 1
    split, both = P("expert", "dp", None), P(("expert", "dp"), None)

    def whole(tokens, out_grad, expert_ids, gates, w_gate, w_up, w_down):
        tok = tokens.shape[0] // (experts * groups)
        cap = max(2, 3 * tok * expert_ids.shape[1] // (2 * experts))
        return jax.shard_map(
            functools.partial(per_device, line, groups // 2, cap),
            mesh=mesh,
            in_specs=(both, both, both, both, split, split, split),
            out_specs=(both, both, split, split, split),
            check_vma=False,
        )(tokens, out_grad, expert_ids, gates, w_gate, w_up, w_down)

    return whole
```

```python
import functools

import jax
import jax.numpy as jnp
from jax import lax
from jax.experimental import pallas as pl
from jax.experimental.pallas import tpu as pltpu
from jax.sharding import PartitionSpec as P

MESH = pl.DeviceIdType.MESH
LANES = 128


def dot_nn(a, b):
    return lax.dot_general(a, b, (((1,), (0,)), ((), ())), preferred_element_type=jnp.float32)


def dot_nt(a, b):
    return lax.dot_general(a, b, (((1,), (1,)), ((), ())), preferred_element_type=jnp.float32)


def dot_tn(a, b):
    return lax.dot_general(a, b, (((0,), (0,)), ((), ())), preferred_element_type=jnp.float32)


def split_rows(slots):
    return [(lo, lo + 16) for lo in range(0, slots, 16)]


def kernel(
    line, ring, cap,
    tok_ref, grad_ref, ids_ref, gates_ref, wg_ref, wu_ref, wd_ref,
    dtok_ref, dgate_ref, dwg_ref, dwu_ref, dwd_ref,
    meta, rows1, send2, recv2, wbuf, acts, back_out, back_in, home_out, home_in,
    part, sib, plus_out, plus_in, minus_out, minus_in,
    meta_s, meta_r, one_s, one_r, two_s, two_r, w_s, w_r, ws_s, ws_r,
    back_s, back_r, home_s, home_r, sib_s, sib_r, plus_s, plus_r, minus_s, minus_r,
):
    tok, dim = tok_ref.shape
    top = ids_ref.shape[0]
    hid = wg_ref.shape[1]
    slots = line * cap
    shard = wg_ref.shape[0]
    parts = split_rows(slots)
    offsets = sorted(range(line), key=lambda k: (min(k, line - k), k))
    place_of = {k: q for q, k in enumerate(offsets)}

    expert = lax.axis_index("expert")
    dp = lax.axis_index("dp")
    z, c = dp // 2, dp % 2
    stride_a = line - (line - 1) * c
    stride_b = 1 + (line - 1) * c
    y, x = expert // line, expert % line
    a = y * (1 - c) + x * c
    b = x * (1 - c) + y * c

    def on_a(k):
        return (((a + k + line) % line) * stride_a + b * stride_b, dp)

    def on_b(k):
        return (a * stride_a + ((b + k + line) % line) * stride_b, dp)

    def z_at(k):
        return (z + k + ring) % ring

    def on_z(k):
        return (expert, z_at(k) * 2 + c)

    sibling = (expert, z * 2 + 1 - c)
    pending = []

    def remote(src, dst, send, recv, target):
        copy = pltpu.make_async_remote_copy(
            src_ref=src, dst_ref=dst, send_sem=send, recv_sem=recv, device_id=target, device_id_type=MESH
        )
        copy.start()
        pending.append(copy)
        return copy

    barrier = pltpu.get_barrier_semaphore()
    for k in range(1, line):
        pl.semaphore_signal(barrier, inc=1, device_id=on_a(k), device_id_type=MESH)
        pl.semaphore_signal(barrier, inc=1, device_id=on_b(k), device_id_type=MESH)
    for k in range(1, ring):
        pl.semaphore_signal(barrier, inc=1, device_id=on_z(k), device_id_type=MESH)
    pl.semaphore_signal(barrier, inc=1, device_id=sibling, device_id_type=MESH)

    ids_f = ids_ref[...].astype(jnp.float32)
    gates_f = gates_ref[...].astype(jnp.float32)
    meta[0, :, 0:tok] = jnp.concatenate([ids_f, gates_f], axis=0).astype(jnp.bfloat16)
    meta[0, :, tok:] = jnp.zeros((2 * top, LANES - tok), jnp.bfloat16)
    rows1[0, :, 0:dim] = tok_ref[...]
    rows1[0, :, dim:] = grad_ref[...]
    wbuf[z, c, :, 0:hid] = wg_ref[...]
    wbuf[z, c, :, hid : 2 * hid] = wu_ref[...]
    wbuf[z, c, :, 2 * hid :] = wd_ref[...]

    pl.semaphore_wait(barrier, 2 * (line - 1) + ring)

    metas, ones, weights, shared = {}, {}, {}, {}
    for q in range(1, line):
        metas[q] = remote(meta.at[0], meta.at[q], meta_s.at[q], meta_r.at[q], on_a(offsets[q]))

    def send_rows(q, source, target, i=0, lanes=(0, 2 * dim)):
        cut = slice(*lanes)
        ones[q, i] = remote(
            rows1.at[source, :, cut], rows1.at[q, :, cut], one_s.at[q, i], one_r.at[q, i], on_a(target)
        )

    def send_weights(key, k, target, rows=(0, shard)):
        i, cut = len(weights), slice(*rows)
        ref = wbuf.at[z_at(-k), c, cut]
        weights[key] = remote(ref, ref, w_s.at[i], w_r.at[i], on_z(target))

    def share(k):
        i = len(shared)
        ref = wbuf.at[z_at(-k), c]
        shared[k] = remote(ref, ref, ws_s.at[i], ws_r.at[i], sibling)

    near = (1, -1, 2, -2)
    halves = ((0, 2 * dim),)
    for i, lanes in enumerate(halves):
        for k in near:
            send_rows(place_of[k % line], 0, k, i, lanes)
    for k in near:
        send_weights(k, 0, k)
    share(0)

    for q in range(1, line):
        metas[q].wait_recv()
    every = jnp.concatenate([meta[q].astype(jnp.float32)[:, 0:tok] for q in range(line)], axis=1)
    ids_all, gates_all = every[0:top], every[top:]
    total = line * tok
    masks, scales = [], []
    for j in range(line):
        named = (a * stride_a + ((b + j) % line) * stride_b).astype(jnp.float32)
        hit = ids_all == named
        masks.append(jnp.sum(jnp.where(hit, 1.0, 0.0), axis=0, keepdims=True))
        scales.append(jnp.sum(jnp.where(hit, gates_all, 0.0), axis=0, keepdims=True))
    mask = jnp.concatenate(masks, axis=0)
    rows = lax.broadcasted_iota(jnp.int32, (total, total), 0)
    cols = lax.broadcasted_iota(jnp.int32, (total, total), 1)
    earlier = ((rows < cols) & (rows // tok == cols // tok)).astype(jnp.float32).astype(jnp.bfloat16)
    pos = dot_nn(mask.astype(jnp.bfloat16), earlier)
    first = (lax.broadcasted_iota(jnp.int32, (line, total), 1) // tok * cap).astype(jnp.float32)
    place = jnp.where(mask > 0.0, first + pos, -1.0)
    holds = [(lo // cap, -(-hi // cap)) for lo, hi in parts]
    slot_iota = lax.broadcasted_iota(jnp.int32, (slots, total), 0).astype(jnp.float32)
    picks, scaled_picks = [[] for _ in parts], [[] for _ in parts]
    for j in range(line):
        hit = slot_iota == place[j : j + 1]
        pick = jnp.where(hit, 1.0, 0.0)
        scaled_pick = jnp.where(hit, scales[j], 0.0)
        for g, (lo, hi) in enumerate(parts):
            lanes = slice(holds[g][0] * tok, holds[g][1] * tok)
            picks[g].append(pick[lo:hi, lanes].astype(jnp.bfloat16))
            scaled_picks[g].append(scaled_pick[lo:hi, lanes].astype(jnp.bfloat16))
    picks = [jnp.concatenate(p, axis=0) for p in picks]
    scaled_picks = [jnp.concatenate(p, axis=0) for p in scaled_picks]

    twos = {}

    def dispatch(g):
        (lo, hi), (q0, q1) = parts[g], holds[g]
        count = hi - lo
        for col, pick in ((0, picks[g]), (dim, scaled_picks[g])):
            held = rows1[q0:q1, :, col : col + dim].reshape((q1 - q0) * tok, dim)
            out = dot_nn(pick, held).astype(jnp.bfloat16)
            for j in range(line):
                (send2 if j else recv2)[j, lo:hi, col : col + dim] = out[j * count : (j + 1) * count]
        for j in offsets[1:]:
            twos[j, g] = remote(
                send2.at[j, lo:hi], recv2.at[j, lo:hi], two_s.at[j, g], two_r.at[j, g], on_b(j)
            )

    for i in range(len(halves)):
        for k in (1, -1):
            ones[place_of[k % line], i].wait_recv()
    dispatch(0)
    for i, lanes in enumerate(halves):
        for k in (2, -2):
            ones[place_of[k % line], i].wait_recv()
        send_rows(place_of[3], place_of[2], 1, i, lanes)
        send_rows(place_of[-3 % line], place_of[-2 % line], -1, i, lanes)
        if i == 0:
            send_rows(place_of[4], place_of[2], 2, 0, (0, dim))
        if i == len(halves) - 1:
            send_rows(place_of[4], place_of[-2 % line], -2, 1, (dim, 2 * dim))
    for i in range(len(halves)):
        for k in (3, -3):
            ones[place_of[k % line], i].wait_recv()
    dispatch(1)
    for i in range(2):
        ones[place_of[4], i].wait_recv()
    dispatch(2)

    for k in near:
        weights[k].wait_recv()
    send_weights(3, 2, 1)
    send_weights(-3, -2, -1)
    send_weights(4, 2, 2, (0, shard // 2))
    send_weights(-4, -2, -2, (shard // 2, shard))
    for k in near:
        share(k)
    for k in (3, -3, 4, -4):
        weights[k].wait_recv()
    for k in (3, -3, 4):
        share(k)
    for copy in list(shared.values()):
        copy.wait_recv()

    backs = {}

    def expert_rows(g):
        lo, hi = parts[g]
        count = hi - lo
        in_rows = recv2[:, lo:hi, 0:dim].reshape(line * count, dim)
        scaled = recv2[:, lo:hi, dim:].reshape(line * count, dim)
        w_pair = wbuf[:, :, :, 0 : 2 * hid].reshape(dim, 2 * hid)
        w_down = wbuf[:, :, :, 2 * hid :].reshape(dim, hid)
        pre = dot_nn(in_rows, w_pair)
        gate_pre, up_pre = pre[:, 0:hid], pre[:, hid:]
        hid_grad = dot_nn(scaled, w_down)
        sig = jax.nn.sigmoid(gate_pre)
        act = gate_pre * sig
        hidden = (act * up_pre).astype(jnp.bfloat16)
        score = jnp.sum(hidden.astype(jnp.float32) * hid_grad, axis=1, keepdims=True)
        gate_grad = (hid_grad * up_pre * sig * (1.0 + gate_pre * (1.0 - sig))).astype(jnp.bfloat16)
        up_grad = (hid_grad * act).astype(jnp.bfloat16)
        pair = jnp.concatenate([gate_grad, up_grad], axis=1)
        acts[:, lo:hi, 0 : 2 * hid] = pair.reshape(line, count, 2 * hid)
        acts[:, lo:hi, 2 * hid :] = hidden.reshape(line, count, hid)
        in_grad = dot_nt(pair, w_pair).astype(jnp.bfloat16)
        lane = lax.broadcasted_iota(jnp.int32, (line * count, LANES), 1)
        score_lanes = jnp.where(lane == expert, score, 0.0).astype(jnp.bfloat16)
        for j in offsets:
            there = back_out if j else back_in
            there[j, lo:hi, 0:dim] = in_grad[j * count : (j + 1) * count]
            there[j, lo:hi, dim:] = score_lanes[j * count : (j + 1) * count]
        for j in offsets[1:]:
            backs[j, g] = remote(
                back_out.at[j, lo:hi], back_in.at[j, lo:hi], back_s.at[j, g], back_r.at[j, g], on_b(-j)
            )

    for g in range(len(parts)):
        for j in range(1, line):
            twos[j, g].wait_recv()
        expert_rows(g)

    ahead, behind = ring // 2, ring - 1 - ring // 2
    targets = sorted(range(-behind, ahead + 1), key=lambda k: (-abs(k), -k))
    pair_grad = acts[:, :, 0 : 2 * hid].reshape(line * slots, 2 * hid)
    hidden = acts[:, :, 2 * hid :].reshape(line * slots, hid)
    sibs = {}
    for i, k in enumerate(targets):
        zt = z_at(k)
        cut = pl.ds(pl.multiple_of(zt * (2 * shard), 2 * shard), 2 * shard)
        cut_grad = pl.ds(pl.multiple_of(dim + zt * (2 * shard), 2 * shard), 2 * shard)
        cols_in = recv2[:, :, cut].reshape(line * slots, 2 * shard)
        cols_scaled = recv2[:, :, cut_grad].reshape(line * slots, 2 * shard)
        part[i, :, :, 0 : 2 * hid] = dot_tn(cols_in, pair_grad).astype(jnp.bfloat16).reshape(2, shard, 2 * hid)
        part[i, :, :, 2 * hid :] = dot_tn(cols_scaled, hidden).astype(jnp.bfloat16).reshape(2, shard, hid)
        sibs[k] = remote(part.at[i, 1 - c], sib.at[i], sib_s.at[i], sib_r.at[i], sibling)

    met = set()

    def chip_sum(k, m):
        i, lanes = targets.index(k), slice(m * hid, (m + 1) * hid)
        if k not in met:
            sibs[k].wait_recv()
            met.add(k)
        return part[i, c, :, lanes].astype(jnp.float32) + sib[i, :, lanes].astype(jnp.float32)

    pluses, minuses = {}, {}

    def hop(h, m, k, done, out, inn, send, recv, way):
        value = chip_sum(k, m)
        if h:
            done[h - 1, m].wait_recv()
            value = value + inn[h - 1, m].astype(jnp.float32)
        out[h, m] = value.astype(jnp.bfloat16)
        done[h, m] = remote(out.at[h, m], inn.at[h, m], send.at[h, m], recv.at[h, m], on_z(way))

    def hops(h):
        for m in range(3):
            hop(h, m, ahead - h, pluses, plus_out, plus_in, plus_s, plus_r, 1)
            if h < behind:
                hop(h, m, h - behind, minuses, minus_out, minus_in, minus_s, minus_r, -1)

    homes = {}

    def send_home(q, block):
        (home_out if q else home_in)[q] = block.astype(jnp.bfloat16)
        if q:
            homes[q] = remote(home_out.at[q], home_in.at[q], home_s.at[q], home_r.at[q], on_a(-offsets[q]))

    def combine(g):
        lo, hi = parts[g]
        for j in range(1, line):
            backs[j, g].wait_recv()
        return dot_tn(picks[g], back_in[:, lo:hi].reshape(line * (hi - lo), dim + LANES))

    rest = {}

    def settle(g):
        out, (q0, q1) = combine(g), holds[g]
        ready = holds[g + 1][0] if g + 1 < len(parts) else line
        for q in sorted(range(q0, q1), key=lambda q: -q):
            block = out[(q - q0) * tok : (q - q0 + 1) * tok]
            if q in rest:
                block = block + rest[q]
            if q < ready:
                send_home(q, block)
            else:
                rest[q] = block

    hops(0)
    settle(0)
    settle(1)
    hops(1)
    settle(2)
    for h in range(2, ahead):
        hops(h)

    for q in range(1, line):
        homes[q].wait_recv()
    back = home_in[0].astype(jnp.float32)
    for q in range(1, line):
        back = back + home_in[q].astype(jnp.float32)
    dtok_ref[...] = back[:, 0:dim].astype(jnp.bfloat16)
    eye = (
        lax.broadcasted_iota(jnp.int32, (LANES, LANES), 0) == lax.broadcasted_iota(jnp.int32, (LANES, LANES), 1)
    ).astype(jnp.float32).astype(jnp.bfloat16)
    by_expert = dot_nt(eye, back[:, dim:].astype(jnp.bfloat16))
    expert_iota = lax.broadcasted_iota(jnp.int32, (LANES, tok), 0)
    chosen = [
        jnp.sum(jnp.where(expert_iota == ids_ref[k : k + 1, :], by_expert, 0.0), axis=0, keepdims=True)
        for k in range(top)
    ]
    dgate_ref[...] = (jnp.concatenate(chosen, axis=0) / gates_f).astype(jnp.bfloat16)

    for m, out_ref in enumerate((dwg_ref, dwu_ref, dwd_ref)):
        pluses[ahead - 1, m].wait_recv()
        minuses[behind - 1, m].wait_recv()
        out_ref[...] = (
            chip_sum(0, m) + plus_in[ahead - 1, m].astype(jnp.float32) + minus_in[behind - 1, m].astype(jnp.float32)
        )

    for copy in pending:
        copy.wait_send()


def hand_on(*refs):
    half = len(refs) // 2
    for source, target in zip(refs[:half], refs[half:]):
        target[...] = source[...]


def per_device(line, ring, cap, tokens, out_grad, expert_ids, gates, w_gate, w_up, w_down):
    tok, dim = tokens.shape
    top = expert_ids.shape[1]
    _, shard, hid = w_gate.shape
    slots = line * cap
    ahead, behind = ring // 2, ring - 1 - ring // 2
    bf16, f32 = jnp.bfloat16, jnp.float32
    dma = pltpu.SemaphoreType.DMA
    vmem = pl.BlockSpec(memory_space=pltpu.VMEM)
    shapes = [
        jax.ShapeDtypeStruct((tok, dim), bf16),
        jax.ShapeDtypeStruct((top, tok), bf16),
        jax.ShapeDtypeStruct((shard, hid), f32),
        jax.ShapeDtypeStruct((shard, hid), f32),
        jax.ShapeDtypeStruct((shard, hid), f32),
    ]
    results = pl.pallas_call(
        functools.partial(kernel, line, ring, cap),
        out_shape=[pltpu.VMEM(s.shape, s.dtype) for s in shapes],
        in_specs=[vmem] * 7,
        out_specs=[vmem] * 5,
        scratch_shapes=[
            pltpu.VMEM((line, 2 * top, LANES), bf16),
            pltpu.VMEM((line, tok, 2 * dim), bf16),
            pltpu.VMEM((line, slots, 2 * dim), bf16),
            pltpu.VMEM((line, slots, 2 * dim), bf16),
            pltpu.VMEM((ring, 2, shard, 3 * hid), bf16),
            pltpu.VMEM((line, slots, 3 * hid), bf16),
            pltpu.VMEM((line, slots, dim + LANES), bf16),
            pltpu.VMEM((line, slots, dim + LANES), bf16),
            pltpu.VMEM((line, tok, dim + LANES), bf16),
            pltpu.VMEM((line, tok, dim + LANES), bf16),
            pltpu.VMEM((ring, 2, shard, 3 * hid), bf16),
            pltpu.VMEM((ring, shard, 3 * hid), bf16),
            pltpu.VMEM((ahead, 3, shard, hid), bf16),
            pltpu.VMEM((ahead, 3, shard, hid), bf16),
            pltpu.VMEM((behind, 3, shard, hid), bf16),
            pltpu.VMEM((behind, 3, shard, hid), bf16),
            dma((line,)), dma((line,)), dma((line, 2)), dma((line, 2)), dma((line, 3)), dma((line, 3)),
            dma((ring,)), dma((ring,)), dma((ring,)), dma((ring,)),
            dma((line, 3)), dma((line, 3)), dma((line,)), dma((line,)),
            dma((ring,)), dma((ring,)),
            dma((ahead, 3)), dma((ahead, 3)), dma((behind, 3)), dma((behind, 3)),
        ],
        compiler_params=pltpu.CompilerParams(
            collective_id=0, has_side_effects=True, vmem_limit_bytes=54944 * 1024
        ),
        name="expert_backward",
    )(tokens, out_grad, expert_ids.T, gates.T, w_gate[0], w_up[0], w_down[0])
    d_tokens, d_gates, d_gate_w, d_up_w, d_down_w = pl.pallas_call(
        hand_on, out_shape=shapes, in_specs=[vmem] * 5, out_specs=[vmem] * 5, name="hand_on",
        compiler_params=pltpu.CompilerParams(vmem_limit_bytes=2 * 1024 * 1024),
    )(*results)
    return d_tokens, d_gates.T, d_gate_w[None], d_up_w[None], d_down_w[None]


def solution(mesh):
    experts, groups = mesh.shape["expert"], mesh.shape["dp"]
    line = 1
    while line * line < experts:
        line += 1
    split, both = P("expert", "dp", None), P(("expert", "dp"), None)

    def whole(tokens, out_grad, expert_ids, gates, w_gate, w_up, w_down):
        tok = tokens.shape[0] // (experts * groups)
        cap = max(2, 3 * tok * expert_ids.shape[1] // (2 * experts))
        return jax.shard_map(
            functools.partial(per_device, line, groups // 2, cap),
            mesh=mesh,
            in_specs=(both, both, both, both, split, split, split),
            out_specs=(both, both, split, split, split),
            check_vma=False,
        )(tokens, out_grad, expert_ids, gates, w_gate, w_up, w_down)

    return whole
```

```python
import functools

import jax
import jax.numpy as jnp
from jax import lax
from jax.experimental import pallas as pl
from jax.experimental.pallas import tpu as pltpu
from jax.sharding import PartitionSpec as P

MESH = pl.DeviceIdType.MESH
LANES = 128


def dot_nn(a, b):
    return lax.dot_general(a, b, (((1,), (0,)), ((), ())), preferred_element_type=jnp.float32)


def dot_nt(a, b):
    return lax.dot_general(a, b, (((1,), (1,)), ((), ())), preferred_element_type=jnp.float32)


def dot_tn(a, b):
    return lax.dot_general(a, b, (((0,), (0,)), ((), ())), preferred_element_type=jnp.float32)


def split_rows(slots):
    return [(lo, lo + 16) for lo in range(0, slots, 16)]


def kernel(
    line, ring, cap,
    tok_ref, grad_ref, ids_ref, gates_ref, wg_ref, wu_ref, wd_ref,
    dtok_ref, dgate_ref, dwg_ref, dwu_ref, dwd_ref,
    meta, rows1, send2, recv2, wbuf, acts, back_out, back_in, home_out, home_in,
    early, part, sib, plus_out, plus_in, minus_out, minus_in,
    meta_s, meta_r, one_s, one_r, two_s, two_r, w_s, w_r, ws_s, ws_r,
    back_s, back_r, home_s, home_r, sib_s, sib_r, plus_s, plus_r, minus_s, minus_r,
):
    tok, dim = tok_ref.shape
    top = ids_ref.shape[0]
    hid = wg_ref.shape[1]
    slots = line * cap
    shard = wg_ref.shape[0]
    parts = split_rows(slots)
    offsets = sorted(range(line), key=lambda k: (min(k, line - k), k))
    place_of = {k: q for q, k in enumerate(offsets)}

    expert = lax.axis_index("expert")
    dp = lax.axis_index("dp")
    z, c = dp // 2, dp % 2
    stride_a = line - (line - 1) * c
    stride_b = 1 + (line - 1) * c
    y, x = expert // line, expert % line
    a = y * (1 - c) + x * c
    b = x * (1 - c) + y * c

    def on_a(k):
        return (((a + k + line) % line) * stride_a + b * stride_b, dp)

    def on_b(k):
        return (a * stride_a + ((b + k + line) % line) * stride_b, dp)

    def z_at(k):
        return (z + k + ring) % ring

    def on_z(k):
        return (expert, z_at(k) * 2 + c)

    sibling = (expert, z * 2 + 1 - c)
    pending = []

    def remote(src, dst, send, recv, target):
        copy = pltpu.make_async_remote_copy(
            src_ref=src, dst_ref=dst, send_sem=send, recv_sem=recv, device_id=target, device_id_type=MESH
        )
        copy.start()
        pending.append(copy)
        return copy

    barrier = pltpu.get_barrier_semaphore()
    for k in range(1, line):
        pl.semaphore_signal(barrier, inc=1, device_id=on_a(k), device_id_type=MESH)
        pl.semaphore_signal(barrier, inc=1, device_id=on_b(k), device_id_type=MESH)
    for k in range(1, ring):
        pl.semaphore_signal(barrier, inc=1, device_id=on_z(k), device_id_type=MESH)
    pl.semaphore_signal(barrier, inc=1, device_id=sibling, device_id_type=MESH)

    ids_f = ids_ref[...].astype(jnp.float32)
    gates_f = gates_ref[...].astype(jnp.float32)
    meta[0, :, 0:tok] = jnp.concatenate([ids_f, gates_f], axis=0).astype(jnp.bfloat16)
    meta[0, :, tok:] = jnp.zeros((2 * top, LANES - tok), jnp.bfloat16)
    rows1[0, :, 0:dim] = tok_ref[...]
    rows1[0, :, dim:] = grad_ref[...]
    wbuf[z, c, :, 0:hid] = wg_ref[...]
    wbuf[z, c, :, hid : 2 * hid] = wu_ref[...]
    wbuf[z, c, :, 2 * hid :] = wd_ref[...]

    pl.semaphore_wait(barrier, 2 * (line - 1) + ring)

    metas, ones, weights, shared = {}, {}, {}, {}
    for q in range(1, line):
        metas[q] = remote(meta.at[0], meta.at[q], meta_s.at[q], meta_r.at[q], on_a(offsets[q]))

    def send_rows(q, source, target, i=0, lanes=(0, 2 * dim)):
        cut = slice(*lanes)
        ones[q, i] = remote(
            rows1.at[source, :, cut], rows1.at[q, :, cut], one_s.at[q, i], one_r.at[q, i], on_a(target)
        )

    def send_weights(key, k, target, rows=(0, shard)):
        i, cut = len(weights), slice(*rows)
        ref = wbuf.at[z_at(-k), c, cut]
        weights[key] = remote(ref, ref, w_s.at[i], w_r.at[i], on_z(target))

    def share(k):
        i = len(shared)
        ref = wbuf.at[z_at(-k), c]
        shared[k] = remote(ref, ref, ws_s.at[i], ws_r.at[i], sibling)

    near = (1, -1, 2, -2)
    halves = ((0, 2 * dim),)
    for i, lanes in enumerate(halves):
        for k in near:
            send_rows(place_of[k % line], 0, k, i, lanes)
    for k in near:
        send_weights(k, 0, k)
    share(0)

    for q in range(1, line):
        metas[q].wait_recv()
    every = jnp.concatenate([meta[q].astype(jnp.float32)[:, 0:tok] for q in range(line)], axis=1)
    ids_all, gates_all = every[0:top], every[top:]
    total = line * tok
    masks, scales = [], []
    for j in range(line):
        named = (a * stride_a + ((b + j) % line) * stride_b).astype(jnp.float32)
        hit = ids_all == named
        masks.append(jnp.sum(jnp.where(hit, 1.0, 0.0), axis=0, keepdims=True))
        scales.append(jnp.sum(jnp.where(hit, gates_all, 0.0), axis=0, keepdims=True))
    mask = jnp.concatenate(masks, axis=0)
    rows = lax.broadcasted_iota(jnp.int32, (total, total), 0)
    cols = lax.broadcasted_iota(jnp.int32, (total, total), 1)
    earlier = ((rows < cols) & (rows // tok == cols // tok)).astype(jnp.float32).astype(jnp.bfloat16)
    pos = dot_nn(mask.astype(jnp.bfloat16), earlier)
    first = (lax.broadcasted_iota(jnp.int32, (line, total), 1) // tok * cap).astype(jnp.float32)
    place = jnp.where(mask > 0.0, first + pos, -1.0)
    holds = [(lo // cap, -(-hi // cap)) for lo, hi in parts]
    slot_iota = lax.broadcasted_iota(jnp.int32, (slots, total), 0).astype(jnp.float32)
    picks, scaled_picks = [[] for _ in parts], [[] for _ in parts]
    for j in range(line):
        hit = slot_iota == place[j : j + 1]
        pick = jnp.where(hit, 1.0, 0.0)
        scaled_pick = jnp.where(hit, scales[j], 0.0)
        for g, (lo, hi) in enumerate(parts):
            lanes = slice(holds[g][0] * tok, holds[g][1] * tok)
            picks[g].append(pick[lo:hi, lanes].astype(jnp.bfloat16))
            scaled_picks[g].append(scaled_pick[lo:hi, lanes].astype(jnp.bfloat16))
    picks = [jnp.concatenate(p, axis=0) for p in picks]
    scaled_picks = [jnp.concatenate(p, axis=0) for p in scaled_picks]

    twos = {}

    def dispatch(g):
        (lo, hi), (q0, q1) = parts[g], holds[g]
        count = hi - lo
        for col, pick in ((0, picks[g]), (dim, scaled_picks[g])):
            held = rows1[q0:q1, :, col : col + dim].reshape((q1 - q0) * tok, dim)
            out = dot_nn(pick, held).astype(jnp.bfloat16)
            for j in range(line):
                (send2 if j else recv2)[j, lo:hi, col : col + dim] = out[j * count : (j + 1) * count]
        for j in offsets[1:]:
            twos[j, g] = remote(
                send2.at[j, lo:hi], recv2.at[j, lo:hi], two_s.at[j, g], two_r.at[j, g], on_b(j)
            )

    for i in range(len(halves)):
        for k in (1, -1):
            ones[place_of[k % line], i].wait_recv()
    dispatch(0)
    for i, lanes in enumerate(halves):
        for k in (2, -2):
            ones[place_of[k % line], i].wait_recv()
        send_rows(place_of[3], place_of[2], 1, i, lanes)
        send_rows(place_of[-3 % line], place_of[-2 % line], -1, i, lanes)
        if i == 0:
            send_rows(place_of[4], place_of[2], 2, 0, (0, dim))
        if i == len(halves) - 1:
            send_rows(place_of[4], place_of[-2 % line], -2, 1, (dim, 2 * dim))
    for i in range(len(halves)):
        for k in (3, -3):
            ones[place_of[k % line], i].wait_recv()
    dispatch(1)
    for i in range(2):
        ones[place_of[4], i].wait_recv()
    dispatch(2)

    for k in near:
        weights[k].wait_recv()
    send_weights(3, 2, 1)
    send_weights(-3, -2, -1)
    send_weights(4, 2, 2, (0, shard // 2))
    send_weights(-4, -2, -2, (shard // 2, shard))
    for k in near:
        share(k)
    for k in (3, -3, 4, -4):
        weights[k].wait_recv()
    for k in (3, -3, 4):
        share(k)
    for copy in list(shared.values()):
        copy.wait_recv()

    backs = {}

    def expert_rows(g):
        lo, hi = parts[g]
        count = hi - lo
        in_rows = recv2[:, lo:hi, 0:dim].reshape(line * count, dim)
        scaled = recv2[:, lo:hi, dim:].reshape(line * count, dim)
        w_pair = wbuf[:, :, :, 0 : 2 * hid].reshape(dim, 2 * hid)
        w_down = wbuf[:, :, :, 2 * hid :].reshape(dim, hid)
        pre = dot_nn(in_rows, w_pair)
        gate_pre, up_pre = pre[:, 0:hid], pre[:, hid:]
        hid_grad = dot_nn(scaled, w_down)
        sig = jax.nn.sigmoid(gate_pre)
        act = gate_pre * sig
        hidden = (act * up_pre).astype(jnp.bfloat16)
        score = jnp.sum(hidden.astype(jnp.float32) * hid_grad, axis=1, keepdims=True)
        gate_grad = (hid_grad * up_pre * sig * (1.0 + gate_pre * (1.0 - sig))).astype(jnp.bfloat16)
        up_grad = (hid_grad * act).astype(jnp.bfloat16)
        pair = jnp.concatenate([gate_grad, up_grad], axis=1)
        acts[:, lo:hi, 0 : 2 * hid] = pair.reshape(line, count, 2 * hid)
        acts[:, lo:hi, 2 * hid :] = hidden.reshape(line, count, hid)
        in_grad = dot_nt(pair, w_pair).astype(jnp.bfloat16)
        lane = lax.broadcasted_iota(jnp.int32, (line * count, LANES), 1)
        score_lanes = jnp.where(lane == expert, score, 0.0).astype(jnp.bfloat16)
        for j in offsets:
            there = back_out if j else back_in
            there[j, lo:hi, 0:dim] = in_grad[j * count : (j + 1) * count]
            there[j, lo:hi, dim:] = score_lanes[j * count : (j + 1) * count]
        for j in offsets[1:]:
            backs[j, g] = remote(
                back_out.at[j, lo:hi], back_in.at[j, lo:hi], back_s.at[j, g], back_r.at[j, g], on_b(-j)
            )

    ahead, behind = ring // 2, ring - 1 - ring // 2
    targets = sorted(range(-behind, ahead + 1), key=lambda k: (-abs(k), -k))

    def weight_grads(k, lo, hi):
        at = z_at(k) * (2 * shard)
        cut = pl.ds(pl.multiple_of(at, 2 * shard), 2 * shard)
        cut_grad = pl.ds(pl.multiple_of(dim + at, 2 * shard), 2 * shard)
        count = line * (hi - lo)
        pair = acts[:, lo:hi, 0 : 2 * hid].reshape(count, 2 * hid)
        hidden = acts[:, lo:hi, 2 * hid :].reshape(count, hid)
        return (
            dot_tn(recv2[:, lo:hi, cut].reshape(count, 2 * shard), pair),
            dot_tn(recv2[:, lo:hi, cut_grad].reshape(count, 2 * shard), hidden),
        )

    for g in range(len(parts)):
        for j in range(1, line):
            twos[j, g].wait_recv()
        expert_rows(g)
        if g == 0:
            for i, k in enumerate(targets):
                pair, down = weight_grads(k, *parts[0])
                early[i, :, 0 : 2 * hid] = pair
                early[i, :, 2 * hid :] = down

    sibs = {}
    for i, k in enumerate(targets):
        pair, down = weight_grads(k, parts[1][0], slots)
        pair = (pair + early[i, :, 0 : 2 * hid]).astype(jnp.bfloat16)
        down = (down + early[i, :, 2 * hid :]).astype(jnp.bfloat16)
        part[i, :, :, 0 : 2 * hid] = pair.reshape(2, shard, 2 * hid)
        part[i, :, :, 2 * hid :] = down.reshape(2, shard, hid)
        sibs[k] = remote(part.at[i, 1 - c], sib.at[i], sib_s.at[i], sib_r.at[i], sibling)

    met = set()

    def chip_sum(k, m):
        i, lanes = targets.index(k), slice(m * hid, (m + 1) * hid)
        if k not in met:
            sibs[k].wait_recv()
            met.add(k)
        return part[i, c, :, lanes].astype(jnp.float32) + sib[i, :, lanes].astype(jnp.float32)

    pluses, minuses = {}, {}

    def hop(h, m, k, done, out, inn, send, recv, way):
        value = chip_sum(k, m)
        if h:
            done[h - 1, m].wait_recv()
            value = value + inn[h - 1, m].astype(jnp.float32)
        out[h, m] = value.astype(jnp.bfloat16)
        done[h, m] = remote(out.at[h, m], inn.at[h, m], send.at[h, m], recv.at[h, m], on_z(way))

    def hops(h):
        for m in range(3):
            hop(h, m, ahead - h, pluses, plus_out, plus_in, plus_s, plus_r, 1)
            if h < behind:
                hop(h, m, h - behind, minuses, minus_out, minus_in, minus_s, minus_r, -1)

    homes = {}

    def send_home(q, block):
        (home_out if q else home_in)[q] = block.astype(jnp.bfloat16)
        if q:
            homes[q] = remote(home_out.at[q], home_in.at[q], home_s.at[q], home_r.at[q], on_a(-offsets[q]))

    def combine(g):
        lo, hi = parts[g]
        for j in range(1, line):
            backs[j, g].wait_recv()
        return dot_tn(picks[g], back_in[:, lo:hi].reshape(line * (hi - lo), dim + LANES))

    rest = {}

    def settle(g):
        out, (q0, q1) = combine(g), holds[g]
        ready = holds[g + 1][0] if g + 1 < len(parts) else line
        for q in sorted(range(q0, q1), key=lambda q: -q):
            block = out[(q - q0) * tok : (q - q0 + 1) * tok]
            if q in rest:
                block = block + rest[q]
            if q < ready:
                send_home(q, block)
            else:
                rest[q] = block

    hops(0)
    settle(0)
    settle(1)
    hops(1)
    settle(2)
    for h in range(2, ahead):
        hops(h)

    for q in range(1, line):
        homes[q].wait_recv()
    back = home_in[0].astype(jnp.float32)
    for q in range(1, line):
        back = back + home_in[q].astype(jnp.float32)
    dtok_ref[...] = back[:, 0:dim].astype(jnp.bfloat16)
    eye = (
        lax.broadcasted_iota(jnp.int32, (LANES, LANES), 0) == lax.broadcasted_iota(jnp.int32, (LANES, LANES), 1)
    ).astype(jnp.float32).astype(jnp.bfloat16)
    by_expert = dot_nt(eye, back[:, dim:].astype(jnp.bfloat16))
    expert_iota = lax.broadcasted_iota(jnp.int32, (LANES, tok), 0)
    chosen = [
        jnp.sum(jnp.where(expert_iota == ids_ref[k : k + 1, :], by_expert, 0.0), axis=0, keepdims=True)
        for k in range(top)
    ]
    dgate_ref[...] = (jnp.concatenate(chosen, axis=0) / gates_f).astype(jnp.bfloat16)

    for m, out_ref in enumerate((dwg_ref, dwu_ref, dwd_ref)):
        pluses[ahead - 1, m].wait_recv()
        minuses[behind - 1, m].wait_recv()
        out_ref[...] = (
            chip_sum(0, m) + plus_in[ahead - 1, m].astype(jnp.float32) + minus_in[behind - 1, m].astype(jnp.float32)
        )

    for copy in pending:
        copy.wait_send()


def hand_on(*refs):
    half = len(refs) // 2
    for source, target in zip(refs[:half], refs[half:]):
        target[...] = source[...]


def per_device(line, ring, cap, tokens, out_grad, expert_ids, gates, w_gate, w_up, w_down):
    tok, dim = tokens.shape
    top = expert_ids.shape[1]
    _, shard, hid = w_gate.shape
    slots = line * cap
    ahead, behind = ring // 2, ring - 1 - ring // 2
    bf16, f32 = jnp.bfloat16, jnp.float32
    dma = pltpu.SemaphoreType.DMA
    vmem = pl.BlockSpec(memory_space=pltpu.VMEM)
    shapes = [
        jax.ShapeDtypeStruct((tok, dim), bf16),
        jax.ShapeDtypeStruct((top, tok), bf16),
        jax.ShapeDtypeStruct((shard, hid), f32),
        jax.ShapeDtypeStruct((shard, hid), f32),
        jax.ShapeDtypeStruct((shard, hid), f32),
    ]
    results = pl.pallas_call(
        functools.partial(kernel, line, ring, cap),
        out_shape=[pltpu.VMEM(s.shape, s.dtype) for s in shapes],
        in_specs=[vmem] * 7,
        out_specs=[vmem] * 5,
        scratch_shapes=[
            pltpu.VMEM((line, 2 * top, LANES), bf16),
            pltpu.VMEM((line, tok, 2 * dim), bf16),
            pltpu.VMEM((line, slots, 2 * dim), bf16),
            pltpu.VMEM((line, slots, 2 * dim), bf16),
            pltpu.VMEM((ring, 2, shard, 3 * hid), bf16),
            pltpu.VMEM((line, slots, 3 * hid), bf16),
            pltpu.VMEM((line, slots, dim + LANES), bf16),
            pltpu.VMEM((line, slots, dim + LANES), bf16),
            pltpu.VMEM((line, tok, dim + LANES), bf16),
            pltpu.VMEM((line, tok, dim + LANES), bf16),
            pltpu.VMEM((ring, 2 * shard, 3 * hid), f32),
            pltpu.VMEM((ring, 2, shard, 3 * hid), bf16),
            pltpu.VMEM((ring, shard, 3 * hid), bf16),
            pltpu.VMEM((ahead, 3, shard, hid), bf16),
            pltpu.VMEM((ahead, 3, shard, hid), bf16),
            pltpu.VMEM((behind, 3, shard, hid), bf16),
            pltpu.VMEM((behind, 3, shard, hid), bf16),
            dma((line,)), dma((line,)), dma((line, 2)), dma((line, 2)), dma((line, 3)), dma((line, 3)),
            dma((ring,)), dma((ring,)), dma((ring,)), dma((ring,)),
            dma((line, 3)), dma((line, 3)), dma((line,)), dma((line,)),
            dma((ring,)), dma((ring,)),
            dma((ahead, 3)), dma((ahead, 3)), dma((behind, 3)), dma((behind, 3)),
        ],
        compiler_params=pltpu.CompilerParams(
            collective_id=0, has_side_effects=True, vmem_limit_bytes=54944 * 1024
        ),
        name="expert_backward",
    )(tokens, out_grad, expert_ids.T, gates.T, w_gate[0], w_up[0], w_down[0])
    d_tokens, d_gates, d_gate_w, d_up_w, d_down_w = pl.pallas_call(
        hand_on, out_shape=shapes, in_specs=[vmem] * 5, out_specs=[vmem] * 5, name="hand_on",
        compiler_params=pltpu.CompilerParams(vmem_limit_bytes=2 * 1024 * 1024),
    )(*results)
    return d_tokens, d_gates.T, d_gate_w[None], d_up_w[None], d_down_w[None]


def solution(mesh):
    experts, groups = mesh.shape["expert"], mesh.shape["dp"]
    line = 1
    while line * line < experts:
        line += 1
    split, both = P("expert", "dp", None), P(("expert", "dp"), None)

    def whole(tokens, out_grad, expert_ids, gates, w_gate, w_up, w_down):
        tok = tokens.shape[0] // (experts * groups)
        cap = max(2, 3 * tok * expert_ids.shape[1] // (2 * experts))
        return jax.shard_map(
            functools.partial(per_device, line, groups // 2, cap),
            mesh=mesh,
            in_specs=(both, both, both, both, split, split, split),
            out_specs=(both, both, split, split, split),
            check_vma=False,
        )(tokens, out_grad, expert_ids, gates, w_gate, w_up, w_down)

    return whole
```
